32 devices in a mesh: dp: 4 (over y, x), expert: 8 (over z, core).
Axes of the slice: x: 2, y: 2, z: 4, core: 2. Of those that a mesh axis runs over, the one named last changes fastest.
Arguments:
- tokens: bfloat16 [4096, 768], P(('dp', 'expert')), may hold values from -6 to 6
- expert_ids: int32 [4096, 2], P(('dp', 'expert')), may hold values from 0 to 7, all different within a row; in each aligned block of 128 rows (0 to 127, 128 to 255, ...) at most 64 rows name the same one
- router: bfloat16 [768, 8], replicated, may hold values from -0.4375 to 0.4375
- weight_in: bfloat16 [8, 768, 3072], P('expert'), may hold values from -0.21875 to 0.21875
- weight_out: bfloat16 [8, 3072, 768], P('expert'), may hold values from -0.4375 to 0.4375
- premises: bfloat16 [512, 768], P('dp'), may hold values from -6 to 6
- positive: int32 [64], replicated, may hold values from 0 to 511
- tile_mask: int32 [32, 4], replicated, may hold values 0 or 1
Outputs:
- grad_in: float32 [8, 768, 3072], P('expert', 'dp')
- grad_out: float32 [8, 3072, 768], P('expert', 'dp')
The draws below stay inside these ranges and needn't reach their ends.
Inputs may be any that keep to these rules, and one draw needn't show every extreme that they name: `expert_ids`: among the 128 tokens of one device no expert is named by more than 64 pairs, and one expert is named by exactly 64; the two experts of a token differ.
All inputs are finite; a program needn't handle non-finite values.
Results may differ from the reference program's by a relative error of at most 0.02.
Values may be sent and summed in bfloat16 or wider, within the bound.
A program may use at most 128 MiB of HBM per device.

```python
import math
import jax
import jax.numpy as jnp
import numpy as np
from jax import lax

D = 768
FF = 3072
LEN = 64
TOK_DEV = 128
PREM_DEV = 128
EXPERTS = 8
CAP = 64
SEQ_DEV = 2
TOKENS = 4096
SEQS = 64
PREMISES = 512
N_DP = 4
N_EXPERT = 8


def plant(values, key, smallest, high):
    longest = values.shape.index(max(values.shape))
    spots = []
    for shift in (0, 1):
        where = [jax.random.randint(jax.random.fold_in(key, axis), (), 0, length) for axis, length in enumerate(values.shape)]
        where[longest] = (where[longest] + shift) % values.shape[longest]
        spots.append(tuple(where))
    return values.at[spots[0]].set(smallest).at[spots[1]].set(high)


def spiked(entries, rng, source, target, parts, factor):
    def block_of(axis_at):
        return (jnp.arange(entries.shape[axis_at]) // (entries.shape[axis_at] // parts)).reshape((-1,) + (1,) * (entries.ndim - 1 - axis_at))

    first = jax.random.permutation(rng, parts)[block_of(target)]
    other_side = (block_of(target) + parts // 2) % parts
    return jnp.where((block_of(source) == first) | (block_of(source) == other_side), factor * entries, entries)


def levels(key, extent, pieces, least, top_value):
    factor_of = 1.0
    for dim, parts in pieces:
        draws = jax.random.uniform(jax.random.fold_in(jax.random.fold_in(key, 6), dim), (parts,), jnp.float32, least / len(pieces), top_value / len(pieces))
        factor_of = factor_of * jnp.repeat(jnp.exp(draws), extent[dim] // parts).reshape((-1,) + (1,) * (len(extent) - 1 - dim))
    return factor_of


def deal_out(stream_key, own, number, rows, amount, top, reach, skew):
    ranking = jax.random.permutation(stream_key, amount)
    heavy_load, usual = portions_of(amount, rows * top, reach, skew, True), portions_of(amount, rows * top, reach, skew, False)
    places = jnp.arange(amount)

    def named(sizes, offset_by):
        used = int((sizes > 0).sum())
        fixed = max(1, used // 4)
        shifted = fixed + (places - fixed + offset_by * (used - fixed)) % max(1, amount - fixed)
        return jnp.zeros((amount,), jnp.int32).at[ranking[jnp.where(places < fixed, places, shifted)]].set(jnp.asarray(sizes, jnp.int32))

    sizes = jnp.where(number % 4 == 0, named(heavy_load, number // 4), named(usual, number - number // 4 - 1))
    mixed = jax.random.permutation(jax.random.fold_in(own, 3), amount)
    giver, taker = mixed[0:amount // 2 * 2:2], mixed[1:amount // 2 * 2:2]
    margin = jnp.minimum(sizes[giver] - 1, reach - sizes[taker]) // 2
    margin = jnp.where((giver == ranking[0]) | (taker == ranking[0]) | (sizes[taker] == 0), 0, jnp.maximum(margin, 0))
    shifted = jax.random.randint(jax.random.fold_in(own, 4), (amount // 2,), 0, 1 << 20) % (margin + 1)
    sizes = sizes.at[giver].add(-shifted).at[taker].add(shifted)
    labels = jnp.searchsorted(jnp.cumsum(sizes), jnp.arange(rows * top), side="right").astype(jnp.int32)
    table = labels.reshape(top, rows).T
    table = table[jax.random.permutation(jax.random.fold_in(own, 1), rows)]
    offset_by = jax.random.randint(jax.random.fold_in(own, 2), (rows, 1), 0, top)
    return jnp.take_along_axis(table, (jnp.arange(top)[None, :] + offset_by) % top, axis=1)


def portions_of(number_of, total, bound, slope, full):
    loads = [(1 << 20) // math.isqrt(standing ** slope) + 1 for standing in range(1, number_of + 1)]
    largest = bound if full else min(bound, max(-(-total // number_of), total * loads[0] // sum(loads)))
    least = 1 if total - largest >= number_of - 1 else 0
    given, rest = [largest] + [least] * (number_of - 1), total - largest - least * (number_of - 1)
    while rest > 0:
        movable = [i for i in range(1, number_of) if given[i] < largest] or [i for i in range(1, number_of) if given[i] < bound]
        pool, budget = sum([loads[i] for i in movable]), rest
        for i in movable:
            extra = min(bound - given[i], max(1, budget * loads[i] // pool), rest)
            given[i] = given[i] + extra
            rest = rest - extra
    return np.array(given)


def centred(rng, extent, width, most, pieces=(), kind=jnp.bfloat16):
    gain = levels(rng, extent, pieces, -0.22, 0.18) if pieces else 1.0
    entries = jax.random.normal(rng, extent, jnp.float32) * width * gain
    return jnp.minimum(jnp.maximum(entries, -most), most).astype(kind)


def heavy_noise(own_key, extent, scale, bound, split, heavy, held_as=jnp.bfloat16):
    array = scale * jax.random.normal(own_key, extent, jnp.float32)
    if split:
        array = array * levels(own_key, extent, split, -0.22, 0.18)
    return jnp.clip(spiked(array, jax.random.fold_in(own_key, 3), *heavy), -bound, bound).astype(held_as)


def setup_inputs(seed: int = 0) -> dict:
    key_of = jax.random.split(jax.random.key(seed), 9)
    tokens = heavy_noise(key_of[0], (TOKENS, D), 1.0, 6.0, ((0, 32),), (0, 1, 32, 2.75))
    expert_ids_keys = jax.random.split(jax.random.fold_in(key_of[1], 1), TOKENS // TOK_DEV)
    expert_ids_turns = jax.random.permutation(jax.random.fold_in(key_of[1], 3), TOKENS // TOK_DEV)
    expert_ids = jax.vmap(lambda own, number: deal_out(jax.random.fold_in(key_of[1], 2), own, number, TOK_DEV, EXPERTS, 2, CAP, 2))(expert_ids_keys, expert_ids_turns).reshape((TOKENS, 2))
    router = centred(key_of[2], (D, EXPERTS), (D // 4) ** -0.5, 0.4375)
    weight_in = centred(key_of[3], (EXPERTS, D, FF), D ** -0.5, 0.21875, ((0, 8),))
    weight_out = centred(key_of[4], (EXPERTS, FF, D), (FF // 16) ** -0.5, 0.4375, ((0, 8),))
    premises = centred(key_of[5], (PREMISES, D), 1.0, 6.0, ((0, 4),))
    positive = plant(jax.random.randint(key_of[6], (SEQS,), 0, PREMISES), jax.random.fold_in(key_of[6], 1), 0, PREMISES - 1).astype(jnp.int32)
    tile_mask = plant((jax.random.randint(key_of[7], (N_DP * N_EXPERT, N_DP), 0, 2) < 1).astype(jnp.int32), jax.random.fold_in(key_of[7], 1), 0, 1)
    return dict(tokens=tokens, expert_ids=expert_ids, router=router, weight_in=weight_in, weight_out=weight_out, premises=premises, positive=positive, tile_mask=tile_mask)


SCORE_SCALE = 20.0
LOSS_SCALE = 64.0
EPSILON = 1e-06

def gelu_parts(pre_act):
    inner_arg = 0.7978845608028654 * (pre_act + 0.044715 * pre_act * pre_act * pre_act)
    tangent = jnp.tanh(inner_arg)
    gelu_val = 0.5 * pre_act * (1.0 + tangent)
    slope_val = 0.5 * (1.0 + tangent) + 0.5 * pre_act * (1.0 - tangent * tangent) * 0.7978845608028654 * (1.0 + 0.134145 * pre_act * pre_act)
    return (gelu_val, slope_val)

def route_slots(expert_ids, logits, experts, capacity):
    pick_hot = expert_ids[:, :, None] == jnp.arange(experts, dtype=jnp.int32)[None, None, :]
    picked = lax.optimization_barrier(jnp.sum(jnp.where(pick_hot, logits[:, None, :], jnp.zeros((), logits.dtype)), axis=2))
    gate_wts = jax.nn.sigmoid(picked - picked[:, ::-1]).astype(jnp.bfloat16)
    flat_ids = expert_ids.reshape(-1)
    flat_hot = (flat_ids[:, None] == jnp.arange(experts, dtype=jnp.int32)[None, :]).astype(jnp.int32)
    running = jnp.cumsum(flat_hot, axis=0)
    position = lax.optimization_barrier(jnp.sum(running * flat_hot, axis=1)) - 1
    slot_ids = flat_ids * capacity + position
    return (gate_wts, slot_ids.reshape(expert_ids.shape).astype(jnp.int32))

def contrast_terms(query_vec, key_rows, key_scale, open_mask, pos_hot):
    include = jnp.logical_or(open_mask, pos_hot)
    scores = SCORE_SCALE * lax.dot_general(query_vec, key_rows, (((1,), (1,)), ((), ())), preferred_element_type=jnp.float32) * key_scale[None, :]
    exp_scores = jnp.where(include, jnp.exp(scores), jnp.zeros((), scores.dtype))
    partition = lax.optimization_barrier(jnp.sum(exp_scores, axis=1))
    soft_weight = (exp_scores * key_scale[None, :]).astype(jnp.bfloat16)
    weighted_sum = jnp.dot(soft_weight, key_rows, preferred_element_type=jnp.float32)
    pos_scale = lax.optimization_barrier(jnp.sum(jnp.where(pos_hot, key_scale[None, :], jnp.zeros((), key_scale.dtype)), axis=1))
    pos_vec = jnp.dot(pos_hot.astype(jnp.bfloat16), key_rows, preferred_element_type=jnp.float32) * pos_scale[:, None]
    return (weighted_sum, partition, pos_vec)

def settle(partial_sums):
    rounded = lax.optimization_barrier(partial_sums.astype(jnp.bfloat16))
    return lax.optimization_barrier(jnp.sum(rounded.astype(jnp.float32), axis=0))

def reference(tokens, expert_ids, router, weight_in, weight_out, premises, positive, tile_mask):
    device_count = N_DP * N_EXPERT
    model_width = tokens.shape[1]
    logits = jnp.dot(tokens, router, preferred_element_type=jnp.float32)
    gate_wts, slot_ids = jax.vmap(lambda ids_block, logit_block: route_slots(ids_block, logit_block, EXPERTS, CAP))(expert_ids.reshape(device_count, TOK_DEV, 2), logits.reshape(device_count, TOK_DEV, EXPERTS))
    gate_flat = gate_wts.reshape(-1).astype(jnp.float32)
    sentinel = TOKENS * 2
    pair_ids = jnp.arange(sentinel, dtype=jnp.int32).reshape(device_count, TOK_DEV * 2)
    table = jnp.full((device_count, EXPERTS * CAP), sentinel, dtype=jnp.int32)
    dev_rows = jnp.arange(device_count, dtype=jnp.int32)[:, None]
    table = table.at[dev_rows, slot_ids.reshape(device_count, TOK_DEV * 2)].set(pair_ids)
    table = table.reshape(device_count, EXPERTS, CAP)

    def expert_rows(expert):
        chosen = lax.dynamic_index_in_dim(table, expert, 1, keepdims=False).reshape(-1)
        is_valid = chosen < sentinel
        safe_pair = jnp.where(is_valid, chosen, jnp.zeros((), jnp.int32))
        token_idx = (safe_pair // 2).astype(jnp.int32)
        rows_in = jnp.where(is_valid[:, None], tokens[token_idx], jnp.zeros((), jnp.bfloat16))
        weight = jnp.where(is_valid, gate_flat[safe_pair], jnp.zeros((), gate_flat.dtype))
        return (rows_in, token_idx, weight)

    def forward_expert(moe_sum, expert):
        rows_in, token_idx, weight = expert_rows(expert)
        pre_act = jnp.dot(rows_in, weight_in[expert], preferred_element_type=jnp.float32)
        gelu_val, slope_val = gelu_parts(pre_act)
        result = jnp.dot(gelu_val.astype(jnp.bfloat16), weight_out[expert], preferred_element_type=jnp.float32).astype(jnp.bfloat16)
        moe_sum = moe_sum.at[token_idx].add(weight[:, None] * result.astype(jnp.float32))
        return (moe_sum, None)
    moe_sum, unused = lax.scan(forward_expert, jnp.zeros((TOKENS, model_width), jnp.float32), jnp.arange(EXPERTS, dtype=jnp.int32))
    mixed_out = tokens.astype(jnp.float32) + moe_sum
    pooled = lax.optimization_barrier(jnp.sum(mixed_out.reshape(SEQS, LEN, model_width), axis=1)) / LEN
    row_scale = lax.rsqrt(lax.optimization_barrier(jnp.sum(pooled * pooled, axis=1)) + EPSILON)
    unit_vec = pooled * row_scale[:, None]
    query_vec = unit_vec.astype(jnp.bfloat16)
    key_scale = lax.rsqrt(lax.optimization_barrier(jnp.sum(jnp.square(premises.astype(jnp.float32)), axis=1)) + EPSILON)
    key_index = jnp.arange(PREMISES, dtype=jnp.int32)
    seq_device = (jnp.arange(SEQS, dtype=jnp.int32) // SEQ_DEV).astype(jnp.int32)
    key_open = tile_mask[seq_device[:, None], (key_index // PREM_DEV)[None, :]] == 1
    pos_hot = key_index[None, :] == positive[:, None]
    weighted_sum, partition, pos_vec = contrast_terms(query_vec, premises, key_scale, key_open, pos_hot)
    delta_unit = LOSS_SCALE * SCORE_SCALE * (weighted_sum / partition[:, None] - pos_vec)
    delta_pooled = row_scale[:, None] * (delta_unit - unit_vec * lax.optimization_barrier(jnp.sum(unit_vec * delta_unit, axis=1, keepdims=True)))
    delta_mixed = jnp.repeat(delta_pooled / LEN, LEN, axis=0)
    group_rows = N_EXPERT * CAP

    def backward_expert(expert):
        rows_in, token_idx, weight = expert_rows(expert)
        pre_act = jnp.dot(rows_in, weight_in[expert], preferred_element_type=jnp.float32)
        gelu_val, slope_val = gelu_parts(pre_act)
        hidden = gelu_val.astype(jnp.bfloat16)
        grad_rows = (weight[:, None] * delta_mixed[token_idx]).astype(jnp.bfloat16)
        dhidden = jnp.dot(grad_rows, weight_out[expert].T, preferred_element_type=jnp.float32)
        delta_pre = (dhidden * slope_val).astype(jnp.bfloat16)
        part_out = jnp.einsum('grf,grd->gfd', hidden.reshape(N_DP, group_rows, FF).astype(jnp.float32), grad_rows.reshape(N_DP, group_rows, model_width).astype(jnp.float32))
        out_total = settle(part_out)
        part_in = jnp.einsum('grd,grf->gdf', rows_in.reshape(N_DP, group_rows, model_width).astype(jnp.float32), delta_pre.reshape(N_DP, group_rows, FF).astype(jnp.float32))
        in_total = settle(part_in)
        return (in_total, out_total)
    grad_in, grad_out = lax.map(backward_expert, jnp.arange(EXPERTS, dtype=jnp.int32))
    return (grad_in, grad_out)
```

```python
import jax
import jax.numpy as jnp
from jax import lax
from jax.sharding import PartitionSpec as P

LEN = 64
SCORE_SCALE = 20.0
LOSS_SCALE = 64.0
EPSILON = 1e-06
AXES = ("dp", "expert")


def gelu_parts(pre_act):
    inner_arg = 0.7978845608028654 * (pre_act + 0.044715 * pre_act * pre_act * pre_act)
    tangent = jnp.tanh(inner_arg)
    gelu_val = 0.5 * pre_act * (1.0 + tangent)
    slope_val = 0.5 * (1.0 + tangent) + 0.5 * pre_act * (
        1.0 - tangent * tangent
    ) * 0.7978845608028654 * (1.0 + 0.134145 * pre_act * pre_act)
    return (gelu_val, slope_val)


def gate_map(tokens, expert_ids, router):
    logits = jnp.dot(tokens, router, preferred_element_type=jnp.float32)
    experts = router.shape[1]
    hot = expert_ids[:, :, None] == jnp.arange(experts, dtype=jnp.int32)[None, None, :]
    picked = jnp.sum(jnp.where(hot, logits[:, None, :], 0.0), axis=2)
    gate = jax.nn.sigmoid(picked - picked[:, ::-1])
    return jnp.sum(jnp.where(hot, gate[:, :, None], 0.0), axis=1).T.astype(jnp.bfloat16)


def on_device(tokens, expert_ids, router, weight_in, weight_out, premises, positive, tile_mask):
    bf16, f32 = jnp.bfloat16, jnp.float32
    token_count, width = tokens.shape
    experts = router.shape[1]
    n_dp, n_ex = lax.axis_size("dp"), lax.axis_size("expert")
    blocks = n_dp * n_ex
    capacity = 4 * token_count // n_ex
    ff = weight_in.shape[2] // n_dp
    dp, ex = lax.axis_index("dp"), lax.axis_index("expert")
    device = dp * n_ex + ex
    per_dev = token_count // LEN
    seqs = blocks * per_dev

    gates = lax.all_gather(gate_map(tokens, expert_ids, router), AXES, axis=0)
    all_tokens = lax.all_gather(tokens, AXES, axis=0)
    keys = lax.all_gather(premises, "dp", axis=0, tiled=True)

    gate = lax.dynamic_index_in_dim(gates, ex, 1, keepdims=False)
    named = gate != 0
    upper = (jnp.arange(token_count)[:, None] <= jnp.arange(token_count)[None, :]).astype(bf16)
    place_at = jnp.dot(named.astype(bf16), upper, preferred_element_type=f32).astype(jnp.int32) - 1
    place = jnp.logical_and(
        place_at[:, None, :] == jnp.arange(capacity, dtype=jnp.int32)[None, :, None], named[:, None, :]
    )
    rows = lax.dot_general(
        place.astype(bf16), all_tokens, (((2,), (1,)), ((0,), (0,))), preferred_element_type=f32
    ).astype(bf16).reshape(blocks * capacity, width)
    own_seq = (jnp.arange(token_count) // LEN)[:, None] == jnp.arange(per_dev)[None, :]
    slot_gate = jnp.sum(
        jnp.where(
            jnp.logical_and(place[:, :, :, None], own_seq[None, None]),
            gate.astype(f32)[:, None, :, None],
            0.0,
        ),
        axis=2,
    )
    eye = jnp.eye(blocks, dtype=f32)
    spread = (slot_gate[:, :, None, :] * eye[:, None, :, None]).astype(bf16).reshape(
        blocks * capacity, seqs
    )

    w_in = lax.dynamic_slice_in_dim(weight_in[0], dp * ff, ff, 1)
    w_out = lax.dynamic_slice_in_dim(weight_out[0], dp * ff, ff, 0)
    pre_act = jnp.dot(rows, w_in, preferred_element_type=f32)
    gelu_val, slope_val = gelu_parts(pre_act)
    hidden = gelu_val.astype(bf16)
    seq_hidden = lax.dot_general(
        spread, hidden, (((0,), (0,)), ((), ())), preferred_element_type=f32
    ).astype(bf16)
    partial = jnp.dot(seq_hidden, w_out, preferred_element_type=f32)
    own_sum = jnp.sum(tokens.astype(f32).reshape(per_dev, LEN, width), axis=1)
    mine = (jnp.arange(seqs) // per_dev == device)[:, None]
    partial = partial + jnp.where(mine, jnp.tile(own_sum, (blocks, 1)), 0.0)
    pooled = lax.psum(partial, AXES) / LEN

    row_scale = lax.rsqrt(jnp.sum(pooled * pooled, axis=1) + EPSILON)
    unit = pooled * row_scale[:, None]
    key_scale = lax.rsqrt(jnp.sum(jnp.square(keys.astype(f32)), axis=1) + EPSILON)
    pos_hot = jnp.arange(keys.shape[0], dtype=jnp.int32)[None, :] == positive[:, None]
    key_open = jnp.repeat(jnp.repeat(tile_mask, premises.shape[0], axis=1), per_dev, axis=0) == 1
    include = jnp.logical_or(key_open, pos_hot)
    scores = SCORE_SCALE * lax.dot_general(
        unit.astype(bf16), keys, (((1,), (1,)), ((), ())), preferred_element_type=f32
    ) * key_scale[None, :]
    exp_scores = jnp.where(include, jnp.exp(scores), 0.0)
    partition = jnp.sum(exp_scores, axis=1)
    soft = (exp_scores * key_scale[None, :]).astype(bf16)
    both = jnp.dot(
        jnp.concatenate([soft, pos_hot.astype(bf16)], axis=0), keys, preferred_element_type=f32
    )
    pos_scale = jnp.sum(jnp.where(pos_hot, key_scale[None, :], 0.0), axis=1)
    delta_unit = LOSS_SCALE * SCORE_SCALE * (
        both[:seqs] / partition[:, None] - both[seqs:] * pos_scale[:, None]
    )
    delta = row_scale[:, None] * (
        delta_unit - unit * jnp.sum(unit * delta_unit, axis=1, keepdims=True)
    )
    delta = (delta / LEN).astype(bf16)

    grad_out = lax.dot_general(
        seq_hidden, delta, (((0,), (0,)), ((), ())), preferred_element_type=f32
    )
    seq_dh = lax.dot_general(
        delta, w_out, (((1,), (1,)), ((), ())), preferred_element_type=f32
    ).astype(bf16)
    delta_pre = (jnp.dot(spread, seq_dh, preferred_element_type=f32) * slope_val).astype(bf16)
    grad_in = lax.dot_general(
        rows, delta_pre, (((0,), (0,)), ((), ())), preferred_element_type=f32
    ).astype(bf16)
    grad_in = lax.all_to_all(grad_in, "dp", split_axis=0, concat_axis=1, tiled=True)
    return (grad_in.astype(f32)[None], grad_out[None])


def solution(mesh):
    in_specs = (
        P(AXES, None),
        P(AXES, None),
        P(),
        P("expert", None, None),
        P("expert", None, None),
        P("dp", None),
        P(),
        P(),
    )
    out_specs = (P("expert", "dp", None), P("expert", "dp", None))
    return jax.shard_map(
        on_device, mesh=mesh, in_specs=in_specs, out_specs=out_specs, check_vma=False
    )
```

```python
import functools

import jax
import jax.numpy as jnp
from jax import lax
from jax.experimental import pallas as pl
from jax.experimental.pallas import tpu as pltpu
from jax.sharding import PartitionSpec as P

LEN = 64
SCORE_SCALE = 20.0
LOSS_SCALE = 64.0
EPSILON = 1e-06
AXES = ("dp", "expert")


def gelu_parts(pre_act):
    inner_arg = 0.7978845608028654 * (pre_act + 0.044715 * pre_act * pre_act * pre_act)
    tangent = jnp.tanh(inner_arg)
    gelu_val = 0.5 * pre_act * (1.0 + tangent)
    slope_val = 0.5 * (1.0 + tangent) + 0.5 * pre_act * (
        1.0 - tangent * tangent
    ) * 0.7978845608028654 * (1.0 + 0.134145 * pre_act * pre_act)
    return (gelu_val, slope_val)


MESH = pl.DeviceIdType.MESH


def greet_all(n_ex, blocks, me):
    barrier = pltpu.get_barrier_semaphore()

    def hello(d, _):
        t = lax.rem(me + d, blocks)
        pl.semaphore_signal(barrier, inc=1, device_id=(t // n_ex, lax.rem(t, n_ex)), device_id_type=MESH)
        return 0

    lax.fori_loop(1, blocks, hello, 0)
    pl.semaphore_wait(barrier, blocks - 1)


def gather_kernel(n_dp, n_ex, tok, tok_v, ids, router, prem, all_tok, gates, keys,
                  gmap, local_sem, send_sem, core_sem, recv_sem, gsend_sem, grecv_sem, psend_sem, precv_sem):
    blocks, nz = n_dp * n_ex, n_ex // 2
    i, e = lax.axis_index("dp"), lax.axis_index("expert")
    z, c = e // 2, lax.rem(e, 2)
    me, other = i * n_ex + e, z * 2 + (1 - c)

    def at_block(ii, zz, cc):
        return ii * n_ex + zz * 2 + cc

    def move(src, block, sem, device):
        return pltpu.make_async_remote_copy(
            src_ref=src, dst_ref=all_tok.at[block], send_sem=sem, recv_sem=recv_sem.at[block],
            device_id=device, device_id_type=MESH)

    greet_all(n_ex, blocks, me)

    own = pltpu.make_async_copy(tok, all_tok.at[me], local_sem.at[0])
    own.start()
    own_keys = pltpu.make_async_copy(prem, keys.at[i], local_sem.at[1])
    own_keys.start()

    def own_dp(d, _):
        move(tok, me, send_sem.at[0, d], (lax.rem(i + d, n_dp), e)).start()
        return 0

    def own_z(k, _):
        move(tok, me, send_sem.at[k, 0], (i, lax.rem(z + k, nz) * 2 + c)).start()
        return 0

    lax.fori_loop(1, n_dp, own_dp, 0)
    lax.fori_loop(1, nz, own_z, 0)
    move(tok, me, core_sem.at[me], (i, other)).start()

    experts = router.shape[0]
    logits = lax.dot_general(
        router[...], tok_v[...], (((1,), (1,)), ((), ())), preferred_element_type=jnp.float32)
    lane = lax.broadcasted_iota(jnp.int32, logits.shape, 0)
    hot0, hot1 = lane == ids[0:1, :], lane == ids[1:2, :]
    picked0 = jnp.sum(jnp.where(hot0, logits, 0.0), axis=0, keepdims=True)
    picked1 = jnp.sum(jnp.where(hot1, logits, 0.0), axis=0, keepdims=True)
    gate0, gate1 = jax.nn.sigmoid(picked0 - picked1), jax.nn.sigmoid(picked1 - picked0)
    table = jnp.where(hot0, gate0, jnp.where(hot1, gate1, 0.0)).astype(jnp.bfloat16).astype(jnp.float32)
    for k in range(experts):
        gmap[k] = jnp.broadcast_to(table[k:k + 1, :], gmap.shape[1:])

    def gate_copy(d):
        t = lax.rem(me + d, blocks)
        return pltpu.make_async_remote_copy(
            src_ref=gmap.at[lax.rem(t, n_ex)], dst_ref=gates.at[me], send_sem=gsend_sem.at[d],
            recv_sem=grecv_sem.at[me], device_id=(t // n_ex, lax.rem(t, n_ex)), device_id_type=MESH)

    def gate_start(d, _):
        gate_copy(d).start()
        return 0

    lax.fori_loop(1, blocks, gate_start, 0)
    own_gate = pltpu.make_async_copy(gmap.at[e], gates.at[me], local_sem.at[2])
    own_gate.start()

    def from_z(k, _):
        block = at_block(i, lax.rem(z + k, nz), c)
        move(tok, block, send_sem.at[0, 0], (i, e)).wait_recv()

        def on(d, _):
            move(all_tok.at[block], block, send_sem.at[k, d], (lax.rem(i + d, n_dp), e)).start()
            return 0

        lax.fori_loop(1, n_dp, on, 0)
        move(all_tok.at[block], block, core_sem.at[block], (i, other)).start()
        return 0

    lax.fori_loop(1, nz, from_z, 0)

    def half(src, row, part, sem, device):
        return pltpu.make_async_remote_copy(
            src_ref=src, dst_ref=keys.at[row, part], send_sem=psend_sem.at[sem],
            recv_sem=precv_sem.at[row, part], device_id=device, device_id_type=MESH)

    def own_half(d, _):
        half(prem.at[c], i, c, d, (lax.rem(i + d, n_dp), e)).start()
        return 0

    lax.fori_loop(1, n_dp, own_half, 0)

    def from_dp(n, _):
        k, d = n // (n_dp - 1), 1 + lax.rem(n, n_dp - 1)
        block = at_block(lax.rem(i + d, n_dp), lax.rem(z + k, nz), c)
        move(tok, block, send_sem.at[0, 0], (i, e)).wait_recv()
        move(all_tok.at[block], block, core_sem.at[block], (i, other)).start()
        return 0

    lax.fori_loop(0, nz * (n_dp - 1), from_dp, 0)

    def hand_half(d, _):
        row = lax.rem(i + d, n_dp)
        half(prem.at[c], row, c, d, (i, e)).wait_recv()
        half(keys.at[row, c], row, c, n_dp + d, (i, other)).start()
        return 0

    lax.fori_loop(1, n_dp, hand_half, 0)

    own.wait()
    own_keys.wait()
    own_gate.wait()

    def end_core(n, _):
        ii, zz = n // nz, lax.rem(n, nz)
        move(tok, at_block(ii, zz, 1 - c), send_sem.at[0, 0], (i, e)).wait_recv()
        move(tok, me, core_sem.at[at_block(ii, zz, c)], (i, e)).wait_send()
        return 0

    lax.fori_loop(0, n_dp * nz, end_core, 0)

    def end_send(n, _):
        move(tok, me, send_sem.at[n // n_dp, lax.rem(n, n_dp)], (i, e)).wait_send()
        return 0

    lax.fori_loop(1, nz * n_dp, end_send, 0)

    def end_half(d, _):
        half(prem.at[c], lax.rem(i + d, n_dp), 1 - c, d, (i, e)).wait_recv()
        half(prem.at[c], i, c, d, (i, e)).wait_send()
        half(prem.at[c], i, c, n_dp + d, (i, e)).wait_send()
        return 0

    lax.fori_loop(1, n_dp, end_half, 0)

    def end_gate(d, _):
        s = lax.rem(me + d, blocks)
        gate_copy(d).wait_send()
        pltpu.make_async_remote_copy(
            src_ref=gmap.at[0], dst_ref=gates.at[s], send_sem=gsend_sem.at[d],
            recv_sem=grecv_sem.at[s], device_id=(i, e), device_id_type=MESH).wait_recv()
        return 0

    lax.fori_loop(1, blocks, end_gate, 0)


def gather(n_dp, n_ex, tokens, ids, router, premises):
    blocks = n_dp * n_ex
    tok, width = tokens.shape
    prem = premises.reshape(2, premises.shape[0] // 2, width)
    any_spec, vmem = pl.BlockSpec(memory_space=pl.ANY), pl.BlockSpec(memory_space=pltpu.VMEM)
    dma = pltpu.SemaphoreType.DMA
    return pl.pallas_call(
        functools.partial(gather_kernel, n_dp, n_ex),
        out_shape=(
            jax.ShapeDtypeStruct((blocks, tok, width), tokens.dtype),
            jax.ShapeDtypeStruct((blocks, 8, tok), jnp.float32),
            jax.ShapeDtypeStruct((n_dp,) + prem.shape, premises.dtype),
        ),
        in_specs=[any_spec, vmem, vmem, vmem, any_spec],
        out_specs=(any_spec, any_spec, any_spec),
        scratch_shapes=[
            pltpu.VMEM((router.shape[1], 8, tok), jnp.float32),
            dma((3,)), dma((n_ex // 2, n_dp)), dma((blocks,)), dma((blocks,)),
            dma((blocks,)), dma((blocks,)), dma((2 * n_dp,)), dma((n_dp, 2)),
        ],
        compiler_params=pltpu.CompilerParams(collective_id=0, has_side_effects=True),
    )(tokens, tokens, ids.T, router.T, prem)


def loss_kernel(n_dp, n_ex, partial, own_sum, keys, key_scale, include, pos_hot, out,
                inbox, ssend, srecv, gsend, grecv):
    blocks = n_dp * n_ex
    i, e = lax.axis_index("dp"), lax.axis_index("expert")
    me = i * n_ex + e
    per_dev, width = own_sum.shape

    def copy(src, dst, slot, send, recv, t, s):
        return pltpu.make_async_remote_copy(
            src_ref=src, dst_ref=dst.at[slot], send_sem=send.at[s], recv_sem=recv.at[slot],
            device_id=(t // n_ex, lax.rem(t, n_ex)), device_id_type=MESH)

    greet_all(n_ex, blocks, me)

    def scatter(d, _):
        t = lax.rem(me + d, blocks)
        copy(partial.at[t], inbox, me, ssend, srecv, t, d).start()
        return 0

    lax.fori_loop(1, blocks, scatter, 0)

    def collect(d, total):
        s = lax.rem(me + d, blocks)
        copy(partial.at[me], inbox, s, ssend, srecv, me, d).wait_recv()
        return total + inbox[s]

    total = lax.fori_loop(1, blocks, collect, partial[me] + own_sum[...])
    pad = include.shape[0]
    pooled = jnp.concatenate([total, jnp.zeros((pad - per_dev, width), jnp.float32)], axis=0) / LEN
    row_scale = lax.rsqrt(jnp.sum(pooled * pooled, axis=1, keepdims=True) + EPSILON)
    unit = pooled * row_scale
    rows = keys[...]
    scores = SCORE_SCALE * lax.dot_general(
        unit.astype(jnp.bfloat16), rows, (((1,), (1,)), ((), ())), preferred_element_type=jnp.float32
    ) * key_scale[...]
    exp_scores = jnp.where(include[...] > 0, jnp.exp(scores), 0.0)
    partition = jnp.sum(exp_scores, axis=1, keepdims=True)
    soft = (exp_scores * key_scale[...]).astype(jnp.bfloat16)
    weighted = jnp.dot(soft, rows, preferred_element_type=jnp.float32)
    hot = pos_hot[...]
    pos_vec = jnp.dot(hot.astype(jnp.bfloat16), rows, preferred_element_type=jnp.float32)
    pos_scale = jnp.sum(hot * key_scale[...], axis=1, keepdims=True)
    delta_unit = LOSS_SCALE * SCORE_SCALE * (weighted / partition - pos_vec * pos_scale)
    delta = row_scale * (delta_unit - unit * jnp.sum(unit * delta_unit, axis=1, keepdims=True))
    out[me] = delta[:per_dev] / LEN

    def spread(d, _):
        t = lax.rem(me + d, blocks)
        copy(out.at[me], out, me, gsend, grecv, t, d).start()
        return 0

    lax.fori_loop(1, blocks, spread, 0)

    def end(d, _):
        s = lax.rem(me + d, blocks)
        copy(out.at[me], out, s, gsend, grecv, me, d).wait_recv()
        copy(out.at[me], out, me, gsend, grecv, s, d).wait_send()
        copy(partial.at[s], inbox, me, ssend, srecv, s, d).wait_send()
        return 0

    lax.fori_loop(1, blocks, end, 0)


def loss_grads(n_dp, n_ex, partial, own_sum, keys, key_scale, include, pos_hot):
    blocks = n_dp * n_ex
    vmem = pl.BlockSpec(memory_space=pltpu.VMEM)
    dma = pltpu.SemaphoreType.DMA
    return pl.pallas_call(
        functools.partial(loss_kernel, n_dp, n_ex),
        out_shape=jax.ShapeDtypeStruct(partial.shape, jnp.float32),
        in_specs=[vmem] * 6,
        out_specs=vmem,
        scratch_shapes=[
            pltpu.VMEM(partial.shape, jnp.float32),
            dma((blocks,)), dma((blocks,)), dma((blocks,)), dma((blocks,)),
        ],
        compiler_params=pltpu.CompilerParams(
            collective_id=1, has_side_effects=True, vmem_limit_bytes=48 * 1024 * 1024),
    )(partial, own_sum, keys, key_scale, include, pos_hot)


def on_device(tokens, expert_ids, router, weight_in, weight_out, premises, positive, tile_mask):
    bf16, f32 = jnp.bfloat16, jnp.float32
    token_count, width = tokens.shape
    n_dp, n_ex = lax.axis_size("dp"), lax.axis_size("expert")
    blocks = n_dp * n_ex
    capacity = 4 * token_count // n_ex
    ff = weight_in.shape[2] // n_dp
    dp, ex = lax.axis_index("dp"), lax.axis_index("expert")
    device = dp * n_ex + ex
    per_dev = token_count // LEN
    seqs = blocks * per_dev

    all_tokens, gates, keys = gather(n_dp, n_ex, tokens, expert_ids, router, premises)
    keys = keys.reshape(n_dp * premises.shape[0], width)

    gate = gates[:, 0, :]
    named = gate != 0
    upper = (jnp.arange(token_count)[:, None] <= jnp.arange(token_count)[None, :]).astype(bf16)
    place_at = jnp.dot(named.astype(bf16), upper, preferred_element_type=f32).astype(jnp.int32) - 1
    place = jnp.logical_and(
        place_at[:, None, :] == jnp.arange(capacity, dtype=jnp.int32)[None, :, None], named[:, None, :]
    )
    rows = lax.dot_general(
        place.astype(bf16), all_tokens, (((2,), (1,)), ((0,), (0,))), preferred_element_type=f32
    ).astype(bf16).reshape(blocks * capacity, width)
    own_seq = (jnp.arange(token_count) // LEN)[:, None] == jnp.arange(per_dev)[None, :]
    slot_gate = jnp.sum(
        jnp.where(
            jnp.logical_and(place[:, :, :, None], own_seq[None, None]),
            gate[:, None, :, None],
            0.0,
        ),
        axis=2,
    )
    eye = jnp.eye(blocks, dtype=f32)
    spread = (slot_gate[:, :, None, :] * eye[:, None, :, None]).astype(bf16).reshape(
        blocks * capacity, seqs
    )

    w_in = lax.dynamic_slice_in_dim(weight_in[0], dp * ff, ff, 1)
    w_out = lax.dynamic_slice_in_dim(weight_out[0], dp * ff, ff, 0)
    pre_act = jnp.dot(rows, w_in, preferred_element_type=f32)
    gelu_val, slope_val = gelu_parts(pre_act)
    hidden = gelu_val.astype(bf16)
    seq_hidden = lax.dot_general(
        spread, hidden, (((0,), (0,)), ((), ())), preferred_element_type=f32
    ).astype(bf16)
    partial = jnp.dot(seq_hidden, w_out, preferred_element_type=f32)
    own_sum = jnp.sum(tokens.astype(f32).reshape(per_dev, LEN, width), axis=1)
    key_scale = lax.rsqrt(jnp.sum(jnp.square(keys.astype(f32)), axis=1) + EPSILON)
    own_positive = lax.dynamic_slice_in_dim(positive, device * per_dev, per_dev)
    mask_row = lax.dynamic_index_in_dim(tile_mask, device, 0, keepdims=False)
    pos_hot = jnp.arange(keys.shape[0], dtype=jnp.int32)[None, :] == own_positive[:, None]
    include = jnp.logical_or(jnp.repeat(mask_row, premises.shape[0])[None, :] == 1, pos_hot)
    fill = ((0, 16 - per_dev), (0, 0))
    delta = loss_grads(
        n_dp, n_ex, partial.reshape(blocks, per_dev, width), own_sum, keys, key_scale[None, :],
        jnp.pad(include.astype(f32), fill), jnp.pad(pos_hot.astype(f32), fill),
    ).reshape(seqs, width).astype(bf16)

    grad_out = lax.dot_general(
        seq_hidden, delta, (((0,), (0,)), ((), ())), preferred_element_type=f32
    )
    seq_dh = lax.dot_general(
        delta, w_out, (((1,), (1,)), ((), ())), preferred_element_type=f32
    ).astype(bf16)
    delta_pre = (jnp.dot(spread, seq_dh, preferred_element_type=f32) * slope_val).astype(bf16)
    grad_in = lax.dot_general(
        rows, delta_pre, (((0,), (0,)), ((), ())), preferred_element_type=f32
    ).astype(bf16)
    grad_in = lax.all_to_all(grad_in, "dp", split_axis=0, concat_axis=1, tiled=True)
    return (grad_in.astype(f32)[None], grad_out[None])


def solution(mesh):
    in_specs = (
        P(AXES, None),
        P(AXES, None),
        P(),
        P("expert", None, None),
        P("expert", None, None),
        P("dp", None),
        P(),
        P(),
    )
    out_specs = (P("expert", "dp", None), P("expert", "dp", None))
    return jax.shard_map(
        on_device, mesh=mesh, in_specs=in_specs, out_specs=out_specs, check_vma=False
    )
```

```python
import functools

import jax
import jax.numpy as jnp
from jax import lax
from jax.experimental import pallas as pl
from jax.experimental.pallas import tpu as pltpu
from jax.sharding import PartitionSpec as P

LEN = 64
SCORE_SCALE = 20.0
LOSS_SCALE = 64.0
EPSILON = 1e-06
AXES = ("dp", "expert")


def gelu_parts(pre_act):
    inner_arg = 0.7978845608028654 * (pre_act + 0.044715 * pre_act * pre_act * pre_act)
    tangent = jnp.tanh(inner_arg)
    gelu_val = 0.5 * pre_act * (1.0 + tangent)
    slope_val = 0.5 * (1.0 + tangent) + 0.5 * pre_act * (
        1.0 - tangent * tangent
    ) * 0.7978845608028654 * (1.0 + 0.134145 * pre_act * pre_act)
    return (gelu_val, slope_val)


MESH = pl.DeviceIdType.MESH


def greet_all(n_ex, blocks, me):
    barrier = pltpu.get_barrier_semaphore()

    def hello(d, _):
        t = lax.rem(me + d, blocks)
        pl.semaphore_signal(barrier, inc=1, device_id=(t // n_ex, lax.rem(t, n_ex)), device_id_type=MESH)
        return 0

    lax.fori_loop(1, blocks, hello, 0)
    pl.semaphore_wait(barrier, blocks - 1)


def gather_kernel(n_dp, n_ex, tok, tok_v, ids, router, prem, all_tok, gates, keys,
                  gmap, local_sem, send_sem, core_sem, recv_sem, gsend_sem, grecv_sem, psend_sem, precv_sem):
    blocks, nz = n_dp * n_ex, n_ex // 2
    i, e = lax.axis_index("dp"), lax.axis_index("expert")
    z, c = e // 2, lax.rem(e, 2)
    me, other = i * n_ex + e, z * 2 + (1 - c)

    def at_block(ii, zz, cc):
        return ii * n_ex + zz * 2 + cc

    def move(src, block, sem, device):
        return pltpu.make_async_remote_copy(
            src_ref=src, dst_ref=all_tok.at[block], send_sem=sem, recv_sem=recv_sem.at[block],
            device_id=device, device_id_type=MESH)

    greet_all(n_ex, blocks, me)

    own = pltpu.make_async_copy(tok, all_tok.at[me], local_sem.at[0])
    own.start()
    own_keys = pltpu.make_async_copy(prem, keys.at[i], local_sem.at[1])
    own_keys.start()

    def own_dp(d, _):
        move(tok, me, send_sem.at[0, d], (lax.rem(i + d, n_dp), e)).start()
        return 0

    def own_z(k, _):
        move(tok, me, send_sem.at[k, 0], (i, lax.rem(z + k, nz) * 2 + c)).start()
        return 0

    lax.fori_loop(1, n_dp, own_dp, 0)
    lax.fori_loop(1, nz, own_z, 0)
    move(tok, me, core_sem.at[me], (i, other)).start()

    experts = router.shape[0]
    logits = lax.dot_general(
        router[...], tok_v[...], (((1,), (1,)), ((), ())), preferred_element_type=jnp.float32)
    lane = lax.broadcasted_iota(jnp.int32, logits.shape, 0)
    hot0, hot1 = lane == ids[0:1, :], lane == ids[1:2, :]
    picked0 = jnp.sum(jnp.where(hot0, logits, 0.0), axis=0, keepdims=True)
    picked1 = jnp.sum(jnp.where(hot1, logits, 0.0), axis=0, keepdims=True)
    gate0, gate1 = jax.nn.sigmoid(picked0 - picked1), jax.nn.sigmoid(picked1 - picked0)
    table = jnp.where(hot0, gate0, jnp.where(hot1, gate1, 0.0)).astype(jnp.bfloat16).astype(jnp.float32)
    for k in range(experts):
        gmap[k] = jnp.broadcast_to(table[k:k + 1, :], gmap.shape[1:])

    def gate_copy(d):
        t = lax.rem(me + d, blocks)
        return pltpu.make_async_remote_copy(
            src_ref=gmap.at[lax.rem(t, n_ex)], dst_ref=gates.at[me], send_sem=gsend_sem.at[d],
            recv_sem=grecv_sem.at[me], device_id=(t // n_ex, lax.rem(t, n_ex)), device_id_type=MESH)

    def gate_start(d, _):
        gate_copy(d).start()
        return 0

    lax.fori_loop(1, blocks, gate_start, 0)
    own_gate = pltpu.make_async_copy(gmap.at[e], gates.at[me], local_sem.at[2])
    own_gate.start()

    def from_z(k, _):
        block = at_block(i, lax.rem(z + k, nz), c)
        move(tok, block, send_sem.at[0, 0], (i, e)).wait_recv()

        def on(d, _):
            move(all_tok.at[block], block, send_sem.at[k, d], (lax.rem(i + d, n_dp), e)).start()
            return 0

        lax.fori_loop(1, n_dp, on, 0)
        move(all_tok.at[block], block, core_sem.at[block], (i, other)).start()
        return 0

    lax.fori_loop(1, nz, from_z, 0)

    def half(src, row, part, sem, device):
        return pltpu.make_async_remote_copy(
            src_ref=src, dst_ref=keys.at[row, part], send_sem=psend_sem.at[sem],
            recv_sem=precv_sem.at[row, part], device_id=device, device_id_type=MESH)

    def own_half(d, _):
        half(prem.at[c], i, c, d, (lax.rem(i + d, n_dp), e)).start()
        return 0

    lax.fori_loop(1, n_dp, own_half, 0)

    def from_dp(n, _):
        k, d = n // (n_dp - 1), 1 + lax.rem(n, n_dp - 1)
        block = at_block(lax.rem(i + d, n_dp), lax.rem(z + k, nz), c)
        move(tok, block, send_sem.at[0, 0], (i, e)).wait_recv()
        move(all_tok.at[block], block, core_sem.at[block], (i, other)).start()
        return 0

    lax.fori_loop(0, nz * (n_dp - 1), from_dp, 0)

    def hand_half(d, _):
        row = lax.rem(i + d, n_dp)
        half(prem.at[c], row, c, d, (i, e)).wait_recv()
        half(keys.at[row, c], row, c, n_dp + d, (i, other)).start()
        return 0

    lax.fori_loop(1, n_dp, hand_half, 0)

    own.wait()
    own_keys.wait()
    own_gate.wait()

    def end_core(n, _):
        ii, zz = n // nz, lax.rem(n, nz)
        move(tok, at_block(ii, zz, 1 - c), send_sem.at[0, 0], (i, e)).wait_recv()
        move(tok, me, core_sem.at[at_block(ii, zz, c)], (i, e)).wait_send()
        return 0

    lax.fori_loop(0, n_dp * nz, end_core, 0)

    def end_send(n, _):
        move(tok, me, send_sem.at[n // n_dp, lax.rem(n, n_dp)], (i, e)).wait_send()
        return 0

    lax.fori_loop(1, nz * n_dp, end_send, 0)

    def end_half(d, _):
        half(prem.at[c], lax.rem(i + d, n_dp), 1 - c, d, (i, e)).wait_recv()
        half(prem.at[c], i, c, d, (i, e)).wait_send()
        half(prem.at[c], i, c, n_dp + d, (i, e)).wait_send()
        return 0

    lax.fori_loop(1, n_dp, end_half, 0)

    def end_gate(d, _):
        s = lax.rem(me + d, blocks)
        gate_copy(d).wait_send()
        pltpu.make_async_remote_copy(
            src_ref=gmap.at[0], dst_ref=gates.at[s], send_sem=gsend_sem.at[d],
            recv_sem=grecv_sem.at[s], device_id=(i, e), device_id_type=MESH).wait_recv()
        return 0

    lax.fori_loop(1, blocks, end_gate, 0)


def gather(n_dp, n_ex, tokens, ids, router, premises):
    blocks = n_dp * n_ex
    tok, width = tokens.shape
    prem = premises.reshape(2, premises.shape[0] // 2, width)
    any_spec, vmem = pl.BlockSpec(memory_space=pl.ANY), pl.BlockSpec(memory_space=pltpu.VMEM)
    dma = pltpu.SemaphoreType.DMA
    return pl.pallas_call(
        functools.partial(gather_kernel, n_dp, n_ex),
        out_shape=(
            jax.ShapeDtypeStruct((blocks, tok, width), tokens.dtype),
            jax.ShapeDtypeStruct((blocks, 8, tok), jnp.float32),
            jax.ShapeDtypeStruct((n_dp,) + prem.shape, premises.dtype),
        ),
        in_specs=[any_spec, vmem, vmem, vmem, any_spec],
        out_specs=(any_spec, any_spec, any_spec),
        scratch_shapes=[
            pltpu.VMEM((router.shape[1], 8, tok), jnp.float32),
            dma((3,)), dma((n_ex // 2, n_dp)), dma((blocks,)), dma((blocks,)),
            dma((blocks,)), dma((blocks,)), dma((2 * n_dp,)), dma((n_dp, 2)),
        ],
        compiler_params=pltpu.CompilerParams(collective_id=0, has_side_effects=True),
    )(tokens, tokens, ids.T, router.T, prem)


def loss_kernel(n_dp, n_ex, partial, own_sum, keys, key_scale, include, pos_hot, out,
                inbox, ssend, srecv, gsend, grecv):
    blocks = n_dp * n_ex
    i, e = lax.axis_index("dp"), lax.axis_index("expert")
    me = i * n_ex + e
    per_dev, width = own_sum.shape

    def copy(src, dst, slot, send, recv, t, s):
        return pltpu.make_async_remote_copy(
            src_ref=src, dst_ref=dst.at[slot], send_sem=send.at[s], recv_sem=recv.at[slot],
            device_id=(t // n_ex, lax.rem(t, n_ex)), device_id_type=MESH)

    greet_all(n_ex, blocks, me)

    def scatter(d, _):
        t = lax.rem(me + d, blocks)
        copy(partial.at[t], inbox, me, ssend, srecv, t, d).start()
        return 0

    lax.fori_loop(1, blocks, scatter, 0)

    def collect(d, total):
        s = lax.rem(me + d, blocks)
        copy(partial.at[me], inbox, s, ssend, srecv, me, d).wait_recv()
        return total + inbox[s]

    total = lax.fori_loop(1, blocks, collect, partial[me] + own_sum[...])
    pad = include.shape[0]
    pooled = jnp.concatenate([total, jnp.zeros((pad - per_dev, width), jnp.float32)], axis=0) / LEN
    row_scale = lax.rsqrt(jnp.sum(pooled * pooled, axis=1, keepdims=True) + EPSILON)
    unit = pooled * row_scale
    rows = keys[...]
    scores = SCORE_SCALE * lax.dot_general(
        unit.astype(jnp.bfloat16), rows, (((1,), (1,)), ((), ())), preferred_element_type=jnp.float32
    ) * key_scale[...]
    exp_scores = jnp.where(include[...] > 0, jnp.exp(scores), 0.0)
    partition = jnp.sum(exp_scores, axis=1, keepdims=True)
    soft = (exp_scores * key_scale[...]).astype(jnp.bfloat16)
    weighted = jnp.dot(soft, rows, preferred_element_type=jnp.float32)
    hot = pos_hot[...]
    pos_vec = jnp.dot(hot.astype(jnp.bfloat16), rows, preferred_element_type=jnp.float32)
    pos_scale = jnp.sum(hot * key_scale[...], axis=1, keepdims=True)
    delta_unit = LOSS_SCALE * SCORE_SCALE * (weighted / partition - pos_vec * pos_scale)
    delta = row_scale * (delta_unit - unit * jnp.sum(unit * delta_unit, axis=1, keepdims=True))
    out[me] = delta[:per_dev] / LEN

    def spread(d, _):
        t = lax.rem(me + d, blocks)
        copy(out.at[me], out, me, gsend, grecv, t, d).start()
        return 0

    lax.fori_loop(1, blocks, spread, 0)

    def end(d, _):
        s = lax.rem(me + d, blocks)
        copy(out.at[me], out, s, gsend, grecv, me, d).wait_recv()
        copy(out.at[me], out, me, gsend, grecv, s, d).wait_send()
        copy(partial.at[s], inbox, me, ssend, srecv, s, d).wait_send()
        return 0

    lax.fori_loop(1, blocks, end, 0)


def loss_grads(n_dp, n_ex, partial, own_sum, keys, key_scale, include, pos_hot):
    blocks = n_dp * n_ex
    vmem = pl.BlockSpec(memory_space=pltpu.VMEM)
    dma = pltpu.SemaphoreType.DMA
    return pl.pallas_call(
        functools.partial(loss_kernel, n_dp, n_ex),
        out_shape=jax.ShapeDtypeStruct(partial.shape, jnp.float32),
        in_specs=[vmem] * 6,
        out_specs=vmem,
        scratch_shapes=[
            pltpu.VMEM(partial.shape, jnp.float32),
            dma((blocks,)), dma((blocks,)), dma((blocks,)), dma((blocks,)),
        ],
        compiler_params=pltpu.CompilerParams(
            collective_id=1, has_side_effects=True, vmem_limit_bytes=48 * 1024 * 1024),
    )(partial, own_sum, keys, key_scale, include, pos_hot)


def exchange_kernel(n_dp, rows, slope, spread, seq_dh, out, turned, part, local_sem, send_sem, recv_sem):
    i, e = lax.axis_index("dp"), lax.axis_index("expert")
    _, parts, keep, wide = out.shape
    total, width = rows.shape
    step = 256

    barrier = pltpu.get_barrier_semaphore()
    for d in range(1, n_dp):
        pl.semaphore_signal(barrier, inc=1, device_id=(lax.rem(i + d, n_dp), e), device_id_type=MESH)

    def turn(n, _):
        at = pl.multiple_of(n * step, step)
        turned[:, pl.ds(at, step)] = rows[pl.ds(at, step), :].T
        return 0

    lax.fori_loop(0, total // step, turn, 0)
    pl.semaphore_wait(barrier, n_dp - 1)

    def copy(f, d, slot):
        t = lax.rem(i + d, n_dp)
        return pltpu.make_async_remote_copy(
            src_ref=part.at[f, pl.ds(pl.multiple_of(t * keep, keep), keep), :],
            dst_ref=out.at[slot, f], send_sem=send_sem.at[f, d], recv_sem=recv_sem.at[f, slot],
            device_id=(t, e), device_id_type=MESH)

    for f in range(parts):
        cols = slice(f * wide, (f + 1) * wide)
        back = jnp.dot(spread[...], seq_dh[:, cols], preferred_element_type=jnp.float32)
        delta_pre = (back * slope[:, cols].astype(jnp.float32)).astype(jnp.bfloat16)
        part[f] = jnp.dot(
            turned[...], delta_pre, preferred_element_type=jnp.float32).astype(jnp.bfloat16)
        for d in range(1, n_dp):
            copy(f, d, i).start()
        pltpu.make_async_copy(
            part.at[f, pl.ds(pl.multiple_of(i * keep, keep), keep), :], out.at[i, f], local_sem.at[f]
        ).start()
    for f in range(parts):
        pltpu.make_async_copy(
            part.at[f, pl.ds(pl.multiple_of(i * keep, keep), keep), :], out.at[i, f], local_sem.at[f]
        ).wait()
        for d in range(1, n_dp):
            copy(f, d, lax.rem(i + d, n_dp)).wait_recv()
            copy(f, d, i).wait_send()


def exchange(n_dp, rows, slope, spread, seq_dh):
    total, width = rows.shape
    ff = slope.shape[1]
    wide = 256 if ff % 256 == 0 else ff
    vmem = pl.BlockSpec(memory_space=pltpu.VMEM)
    dma = pltpu.SemaphoreType.DMA
    out = pl.pallas_call(
        functools.partial(exchange_kernel, n_dp),
        out_shape=jax.ShapeDtypeStruct((n_dp, ff // wide, width // n_dp, wide), jnp.bfloat16),
        in_specs=[vmem] * 4,
        out_specs=vmem,
        scratch_shapes=[
            pltpu.VMEM((width, total), jnp.bfloat16),
            pltpu.VMEM((ff // wide, width, wide), jnp.bfloat16),
            dma((ff // wide,)), dma((ff // wide, n_dp)), dma((ff // wide, n_dp)),
        ],
        compiler_params=pltpu.CompilerParams(
            collective_id=2, has_side_effects=True, vmem_limit_bytes=56 * 1024 * 1024),
    )(rows, slope, spread, seq_dh)
    pieces = [out[j, f] for j in range(n_dp) for f in range(ff // wide)]
    return jnp.concatenate(pieces, axis=1)


def on_device(tokens, expert_ids, router, weight_in, weight_out, premises, positive, tile_mask):
    bf16, f32 = jnp.bfloat16, jnp.float32
    token_count, width = tokens.shape
    n_dp, n_ex = lax.axis_size("dp"), lax.axis_size("expert")
    blocks = n_dp * n_ex
    capacity = 4 * token_count // n_ex
    ff = weight_in.shape[2] // n_dp
    dp, ex = lax.axis_index("dp"), lax.axis_index("expert")
    device = dp * n_ex + ex
    per_dev = token_count // LEN
    seqs = blocks * per_dev

    all_tokens, gates, keys = gather(n_dp, n_ex, tokens, expert_ids, router, premises)
    keys = keys.reshape(n_dp * premises.shape[0], width)

    gate = gates[:, 0, :]
    named = gate != 0
    upper = (jnp.arange(token_count)[:, None] <= jnp.arange(token_count)[None, :]).astype(bf16)
    place_at = jnp.dot(named.astype(bf16), upper, preferred_element_type=f32).astype(jnp.int32) - 1
    place = jnp.logical_and(
        place_at[:, None, :] == jnp.arange(capacity, dtype=jnp.int32)[None, :, None], named[:, None, :]
    )
    rows = lax.dot_general(
        place.astype(bf16), all_tokens, (((2,), (1,)), ((0,), (0,))), preferred_element_type=f32
    ).astype(bf16).reshape(blocks * capacity, width)
    own_seq = (jnp.arange(token_count) // LEN)[:, None] == jnp.arange(per_dev)[None, :]
    slot_gate = jnp.sum(
        jnp.where(
            jnp.logical_and(place[:, :, :, None], own_seq[None, None]),
            gate[:, None, :, None],
            0.0,
        ),
        axis=2,
    )
    eye = jnp.eye(blocks, dtype=f32)
    spread = (slot_gate[:, :, None, :] * eye[:, None, :, None]).astype(bf16).reshape(
        blocks * capacity, seqs
    )

    w_in = lax.dynamic_slice_in_dim(weight_in[0], dp * ff, ff, 1)
    w_out = lax.dynamic_slice_in_dim(weight_out[0], dp * ff, ff, 0)
    pre_act = jnp.dot(rows, w_in, preferred_element_type=f32)
    gelu_val, slope_val = gelu_parts(pre_act)
    hidden, slope = gelu_val.astype(bf16), slope_val.astype(bf16)
    seq_hidden = lax.dot_general(
        spread, hidden, (((0,), (0,)), ((), ())), preferred_element_type=f32
    ).astype(bf16)
    partial = jnp.dot(seq_hidden, w_out, preferred_element_type=f32)
    own_sum = jnp.sum(tokens.astype(f32).reshape(per_dev, LEN, width), axis=1)
    key_scale = lax.rsqrt(jnp.sum(jnp.square(keys.astype(f32)), axis=1) + EPSILON)
    own_positive = lax.dynamic_slice_in_dim(positive, device * per_dev, per_dev)
    mask_row = lax.dynamic_index_in_dim(tile_mask, device, 0, keepdims=False)
    pos_hot = jnp.arange(keys.shape[0], dtype=jnp.int32)[None, :] == own_positive[:, None]
    include = jnp.logical_or(jnp.repeat(mask_row, premises.shape[0])[None, :] == 1, pos_hot)
    fill = ((0, 16 - per_dev), (0, 0))
    delta = loss_grads(
        n_dp, n_ex, partial.reshape(blocks, per_dev, width), own_sum, keys, key_scale[None, :],
        jnp.pad(include.astype(f32), fill), jnp.pad(pos_hot.astype(f32), fill),
    ).reshape(seqs, width).astype(bf16)

    grad_out = lax.dot_general(
        seq_hidden, delta, (((0,), (0,)), ((), ())), preferred_element_type=f32
    )
    seq_dh = lax.dot_general(
        delta, w_out, (((1,), (1,)), ((), ())), preferred_element_type=f32
    ).astype(bf16)
    grad_in = exchange(n_dp, rows, slope, spread, seq_dh)
    return (grad_in.astype(f32)[None], grad_out[None])


def solution(mesh):
    in_specs = (
        P(AXES, None),
        P(AXES, None),
        P(),
        P("expert", None, None),
        P("expert", None, None),
        P("dp", None),
        P(),
        P(),
    )
    out_specs = (P("expert", "dp", None), P("expert", "dp", None))
    return jax.shard_map(
        on_device, mesh=mesh, in_specs=in_specs, out_specs=out_specs, check_vma=False
    )
```

```python
import functools

import jax
import jax.numpy as jnp
from jax import lax
from jax.experimental import pallas as pl
from jax.experimental.pallas import tpu as pltpu
from jax.sharding import PartitionSpec as P

LEN = 64
SCORE_SCALE = 20.0
LOSS_SCALE = 64.0
EPSILON = 1e-06
AXES = ("dp", "expert")


def gelu_parts(pre_act):
    inner_arg = 0.7978845608028654 * (pre_act + 0.044715 * pre_act * pre_act * pre_act)
    tangent = jnp.tanh(inner_arg)
    gelu_val = 0.5 * pre_act * (1.0 + tangent)
    slope_val = 0.5 * (1.0 + tangent) + 0.5 * pre_act * (
        1.0 - tangent * tangent
    ) * 0.7978845608028654 * (1.0 + 0.134145 * pre_act * pre_act)
    return (gelu_val, slope_val)


MESH = pl.DeviceIdType.MESH


def greet_all(n_ex, blocks, me):
    barrier = pltpu.get_barrier_semaphore()

    def hello(d, _):
        t = lax.rem(me + d, blocks)
        pl.semaphore_signal(barrier, inc=1, device_id=(t // n_ex, lax.rem(t, n_ex)), device_id_type=MESH)
        return 0

    lax.fori_loop(1, blocks, hello, 0)
    pl.semaphore_wait(barrier, blocks - 1)


def gather_kernel(n_dp, n_ex, tok, tok_v, ids, router, prem, all_tok, gates, keys,
                  gmap, local_sem, send_sem, core_sem, recv_sem, gsend_sem, grecv_sem, psend_sem, precv_sem,
                  hsend_sem, hrecv_sem):
    blocks, nz = n_dp * n_ex, n_ex // 2
    i, e = lax.axis_index("dp"), lax.axis_index("expert")
    z, c = e // 2, lax.rem(e, 2)
    me, other = i * n_ex + e, z * 2 + (1 - c)

    def at_block(ii, zz, cc):
        return ii * n_ex + zz * 2 + cc

    def move(src, block, sem, device):
        return pltpu.make_async_remote_copy(
            src_ref=src, dst_ref=all_tok.at[block], send_sem=sem, recv_sem=recv_sem.at[block],
            device_id=device, device_id_type=MESH)

    greet_all(n_ex, blocks, me)

    own = pltpu.make_async_copy(tok, all_tok.at[me], local_sem.at[0])
    own.start()
    own_keys = pltpu.make_async_copy(prem, keys.at[i], local_sem.at[1])
    own_keys.start()

    square = n_dp == 4
    peers = 3 if square else n_dp

    def peer(d):
        if not square:
            return lax.rem(i + d, n_dp)
        return (2 - d) * (i + 1 - 2 * lax.rem(i, 2)) + (d - 1) * lax.rem(i + 2, 4)

    def own_dp(d, _):
        move(tok, me, send_sem.at[0, d], (peer(d), e)).start()
        return 0

    def own_z(k, _):
        move(tok, me, send_sem.at[k, 0], (i, lax.rem(z + k, nz) * 2 + c)).start()
        return 0

    lax.fori_loop(1, peers, own_dp, 0)
    lax.fori_loop(1, nz, own_z, 0)
    move(tok, me, core_sem.at[me], (i, other)).start()

    experts = router.shape[0]
    logits = lax.dot_general(
        router[...], tok_v[...], (((1,), (1,)), ((), ())), preferred_element_type=jnp.float32)
    lane = lax.broadcasted_iota(jnp.int32, logits.shape, 0)
    hot0, hot1 = lane == ids[0:1, :], lane == ids[1:2, :]
    picked0 = jnp.sum(jnp.where(hot0, logits, 0.0), axis=0, keepdims=True)
    picked1 = jnp.sum(jnp.where(hot1, logits, 0.0), axis=0, keepdims=True)
    gate0, gate1 = jax.nn.sigmoid(picked0 - picked1), jax.nn.sigmoid(picked1 - picked0)
    table = jnp.where(hot0, gate0, jnp.where(hot1, gate1, 0.0)).astype(jnp.bfloat16).astype(jnp.float32)
    for k in range(experts):
        gmap[k] = jnp.broadcast_to(table[k:k + 1, :], gmap.shape[1:])

    def gate_copy(d):
        t = lax.rem(me + d, blocks)
        return pltpu.make_async_remote_copy(
            src_ref=gmap.at[lax.rem(t, n_ex)], dst_ref=gates.at[me], send_sem=gsend_sem.at[d],
            recv_sem=grecv_sem.at[me], device_id=(t // n_ex, lax.rem(t, n_ex)), device_id_type=MESH)

    def gate_start(d, _):
        gate_copy(d).start()
        return 0

    lax.fori_loop(1, blocks, gate_start, 0)
    own_gate = pltpu.make_async_copy(gmap.at[e], gates.at[me], local_sem.at[2])
    own_gate.start()

    def from_z(k, _):
        block = at_block(i, lax.rem(z + k, nz), c)
        move(tok, block, send_sem.at[0, 0], (i, e)).wait_recv()

        def on(d, _):
            move(all_tok.at[block], block, send_sem.at[k, d], (peer(d), e)).start()
            return 0

        lax.fori_loop(1, peers, on, 0)
        move(all_tok.at[block], block, core_sem.at[block], (i, other)).start()
        return 0

    def half_block(block, part, device, k):
        rows = all_tok.at[block, pl.ds(part * (tok.shape[0] // 2), tok.shape[0] // 2), :]
        return pltpu.make_async_remote_copy(
            src_ref=rows, dst_ref=rows, send_sem=hsend_sem.at[k, part], recv_sem=hrecv_sem.at[block, part],
            device_id=device, device_id_type=MESH)

    def from_dp(n, _):
        k, d = n // (peers - 1), 1 + lax.rem(n, peers - 1)
        block = at_block(peer(d), lax.rem(z + k, nz), c)
        move(tok, block, send_sem.at[0, 0], (i, e)).wait_recv()
        if square:
            half_block(block, d - 1, (peer(3 - d), e), k).start()
        move(all_tok.at[block], block, core_sem.at[block], (i, other)).start()
        return 0

    lax.fori_loop(0, peers - 1, from_dp, 0)
    lax.fori_loop(1, nz, from_z, 0)

    def half(src, row, part, sem, device):
        return pltpu.make_async_remote_copy(
            src_ref=src, dst_ref=keys.at[row, part], send_sem=psend_sem.at[sem],
            recv_sem=precv_sem.at[row, part], device_id=device, device_id_type=MESH)

    def own_half(d, _):
        half(prem.at[c], i, c, d, (lax.rem(i + d, n_dp), e)).start()
        return 0

    lax.fori_loop(1, n_dp, own_half, 0)

    lax.fori_loop(peers - 1, nz * (peers - 1), from_dp, 0)

    def from_diagonal(k, _):
        block = at_block(3 - i, lax.rem(z + k, nz), c)
        half_block(block, 0, (i, e), k).wait_recv()
        half_block(block, 1, (i, e), k).wait_recv()
        move(all_tok.at[block], block, core_sem.at[block], (i, other)).start()
        return 0

    if square:
        lax.fori_loop(0, nz, from_diagonal, 0)

    def hand_half(d, _):
        row = lax.rem(i + d, n_dp)
        half(prem.at[c], row, c, d, (i, e)).wait_recv()
        half(keys.at[row, c], row, c, n_dp + d, (i, other)).start()
        return 0

    lax.fori_loop(1, n_dp, hand_half, 0)

    own.wait()
    own_keys.wait()
    own_gate.wait()

    def end_core(n, _):
        ii, zz = n // nz, lax.rem(n, nz)
        move(tok, at_block(ii, zz, 1 - c), send_sem.at[0, 0], (i, e)).wait_recv()
        move(tok, me, core_sem.at[at_block(ii, zz, c)], (i, e)).wait_send()
        return 0

    lax.fori_loop(0, n_dp * nz, end_core, 0)

    def end_dp(n, _):
        move(tok, me, send_sem.at[n // (peers - 1), 1 + lax.rem(n, peers - 1)], (i, e)).wait_send()
        return 0

    def end_z(k, _):
        move(tok, me, send_sem.at[k, 0], (i, e)).wait_send()
        return 0

    def end_diagonal(k, _):
        half_block(me, 0, (i, e), k).wait_send()
        half_block(me, 1, (i, e), k).wait_send()
        return 0

    lax.fori_loop(0, nz * (peers - 1), end_dp, 0)
    lax.fori_loop(1, nz, end_z, 0)
    if square:
        lax.fori_loop(0, nz, end_diagonal, 0)

    def end_half(d, _):
        half(prem.at[c], lax.rem(i + d, n_dp), 1 - c, d, (i, e)).wait_recv()
        half(prem.at[c], i, c, d, (i, e)).wait_send()
        half(prem.at[c], i, c, n_dp + d, (i, e)).wait_send()
        return 0

    lax.fori_loop(1, n_dp, end_half, 0)

    def end_gate(d, _):
        s = lax.rem(me + d, blocks)
        gate_copy(d).wait_send()
        pltpu.make_async_remote_copy(
            src_ref=gmap.at[0], dst_ref=gates.at[s], send_sem=gsend_sem.at[d],
            recv_sem=grecv_sem.at[s], device_id=(i, e), device_id_type=MESH).wait_recv()
        return 0

    lax.fori_loop(1, blocks, end_gate, 0)


def gather(n_dp, n_ex, tokens, ids, router, premises):
    blocks = n_dp * n_ex
    tok, width = tokens.shape
    prem = premises.reshape(2, premises.shape[0] // 2, width)
    any_spec, vmem = pl.BlockSpec(memory_space=pl.ANY), pl.BlockSpec(memory_space=pltpu.VMEM)
    dma = pltpu.SemaphoreType.DMA
    return pl.pallas_call(
        functools.partial(gather_kernel, n_dp, n_ex),
        out_shape=(
            jax.ShapeDtypeStruct((blocks, tok, width), tokens.dtype),
            jax.ShapeDtypeStruct((blocks, 8, tok), jnp.float32),
            jax.ShapeDtypeStruct((n_dp,) + prem.shape, premises.dtype),
        ),
        in_specs=[any_spec, vmem, vmem, vmem, any_spec],
        out_specs=(any_spec, any_spec, any_spec),
        scratch_shapes=[
            pltpu.VMEM((router.shape[1], 8, tok), jnp.float32),
            dma((3,)), dma((n_ex // 2, n_dp)), dma((blocks,)), dma((blocks,)),
            dma((blocks,)), dma((blocks,)), dma((2 * n_dp,)), dma((n_dp, 2)),
            dma((n_ex // 2, 2)), dma((blocks, 2)),
        ],
        compiler_params=pltpu.CompilerParams(collective_id=0, has_side_effects=True),
    )(tokens, tokens, ids.T, router.T, prem)


def loss_kernel(n_dp, n_ex, partial, own_sum, keys, key_scale, include, pos_hot, out,
                inbox, ssend, srecv, gsend, grecv):
    blocks = n_dp * n_ex
    i, e = lax.axis_index("dp"), lax.axis_index("expert")
    me = i * n_ex + e
    per_dev, width = own_sum.shape

    def copy(src, dst, slot, send, recv, t, s):
        return pltpu.make_async_remote_copy(
            src_ref=src, dst_ref=dst.at[slot], send_sem=send.at[s], recv_sem=recv.at[slot],
            device_id=(t // n_ex, lax.rem(t, n_ex)), device_id_type=MESH)

    greet_all(n_ex, blocks, me)

    def scatter(d, _):
        t = lax.rem(me + d, blocks)
        copy(partial.at[t], inbox, me, ssend, srecv, t, d).start()
        return 0

    lax.fori_loop(1, blocks, scatter, 0)

    def collect(d, total):
        s = lax.rem(me + d, blocks)
        copy(partial.at[me], inbox, s, ssend, srecv, me, d).wait_recv()
        return total + inbox[s]

    total = lax.fori_loop(1, blocks, collect, partial[me] + own_sum[...])
    pad = include.shape[0]
    pooled = jnp.concatenate([total, jnp.zeros((pad - per_dev, width), jnp.float32)], axis=0) / LEN
    row_scale = lax.rsqrt(jnp.sum(pooled * pooled, axis=1, keepdims=True) + EPSILON)
    unit = pooled * row_scale
    rows = keys[...]
    scores = SCORE_SCALE * lax.dot_general(
        unit.astype(jnp.bfloat16), rows, (((1,), (1,)), ((), ())), preferred_element_type=jnp.float32
    ) * key_scale[...]
    exp_scores = jnp.where(include[...] > 0, jnp.exp(scores), 0.0)
    partition = jnp.sum(exp_scores, axis=1, keepdims=True)
    soft = (exp_scores * key_scale[...]).astype(jnp.bfloat16)
    weighted = jnp.dot(soft, rows, preferred_element_type=jnp.float32)
    hot = pos_hot[...]
    pos_vec = jnp.dot(hot.astype(jnp.bfloat16), rows, preferred_element_type=jnp.float32)
    pos_scale = jnp.sum(hot * key_scale[...], axis=1, keepdims=True)
    delta_unit = LOSS_SCALE * SCORE_SCALE * (weighted / partition - pos_vec * pos_scale)
    delta = row_scale * (delta_unit - unit * jnp.sum(unit * delta_unit, axis=1, keepdims=True))
    out[me] = delta[:per_dev] / LEN

    def spread(d, _):
        t = lax.rem(me + d, blocks)
        copy(out.at[me], out, me, gsend, grecv, t, d).start()
        return 0

    lax.fori_loop(1, blocks, spread, 0)

    def end(d, _):
        s = lax.rem(me + d, blocks)
        copy(out.at[me], out, s, gsend, grecv, me, d).wait_recv()
        copy(out.at[me], out, me, gsend, grecv, s, d).wait_send()
        copy(partial.at[s], inbox, me, ssend, srecv, s, d).wait_send()
        return 0

    lax.fori_loop(1, blocks, end, 0)


def loss_grads(n_dp, n_ex, partial, own_sum, keys, key_scale, include, pos_hot):
    blocks = n_dp * n_ex
    vmem = pl.BlockSpec(memory_space=pltpu.VMEM)
    dma = pltpu.SemaphoreType.DMA
    return pl.pallas_call(
        functools.partial(loss_kernel, n_dp, n_ex),
        out_shape=jax.ShapeDtypeStruct(partial.shape, jnp.float32),
        in_specs=[vmem] * 6,
        out_specs=vmem,
        scratch_shapes=[
            pltpu.VMEM(partial.shape, jnp.float32),
            dma((blocks,)), dma((blocks,)), dma((blocks,)), dma((blocks,)),
        ],
        compiler_params=pltpu.CompilerParams(
            collective_id=1, has_side_effects=True, vmem_limit_bytes=48 * 1024 * 1024),
    )(partial, own_sum, keys, key_scale, include, pos_hot)


def exchange_kernel(n_dp, rows, slope, spread, seq_dh, grads, out, turned, part, local_sem, send_sem, recv_sem):
    i, e = lax.axis_index("dp"), lax.axis_index("expert")
    _, parts, keep, wide = out.shape
    total, width = rows.shape
    step = 256

    barrier = pltpu.get_barrier_semaphore()
    for d in range(1, n_dp):
        pl.semaphore_signal(barrier, inc=1, device_id=(lax.rem(i + d, n_dp), e), device_id_type=MESH)

    def turn(n, _):
        at = pl.multiple_of(n * step, step)
        turned[:, pl.ds(at, step)] = rows[pl.ds(at, step), :].T
        return 0

    lax.fori_loop(0, total // step, turn, 0)
    pl.semaphore_wait(barrier, n_dp - 1)

    def copy(f, d, slot):
        t = lax.rem(i + d, n_dp)
        return pltpu.make_async_remote_copy(
            src_ref=part.at[f, pl.ds(pl.multiple_of(t * keep, keep), keep), :],
            dst_ref=out.at[slot, f], send_sem=send_sem.at[f, d], recv_sem=recv_sem.at[f, slot],
            device_id=(t, e), device_id_type=MESH)

    for f in range(parts):
        cols = slice(f * wide, (f + 1) * wide)
        back = jnp.dot(spread[...], seq_dh[:, cols], preferred_element_type=jnp.float32)
        delta_pre = (back * slope[:, cols].astype(jnp.float32)).astype(jnp.bfloat16)
        part[f] = jnp.dot(
            turned[...], delta_pre, preferred_element_type=jnp.float32).astype(jnp.bfloat16)
        for d in range(1, n_dp):
            copy(f, d, i).start()
        pltpu.make_async_copy(
            part.at[f, pl.ds(pl.multiple_of(i * keep, keep), keep), :], out.at[i, f], local_sem.at[f]
        ).start()
    for f in range(parts):
        pltpu.make_async_copy(
            part.at[f, pl.ds(pl.multiple_of(i * keep, keep), keep), :], out.at[i, f], local_sem.at[f]
        ).wait()
        for d in range(1, n_dp):
            copy(f, d, lax.rem(i + d, n_dp)).wait_recv()
        for j in range(n_dp):
            at = (j * parts + f) * wide
            grads[:, at:at + wide] = out[j, f].astype(jnp.float32)
    for f in range(parts):
        for d in range(1, n_dp):
            copy(f, d, i).wait_send()


def exchange(n_dp, rows, slope, spread, seq_dh):
    total, width = rows.shape
    ff = slope.shape[1]
    wide = 256 if ff % 256 == 0 else ff
    vmem = pl.BlockSpec(memory_space=pltpu.VMEM)
    dma = pltpu.SemaphoreType.DMA
    return pl.pallas_call(
        functools.partial(exchange_kernel, n_dp),
        out_shape=jax.ShapeDtypeStruct((width // n_dp, n_dp * ff), jnp.float32),
        in_specs=[vmem] * 4,
        out_specs=vmem,
        scratch_shapes=[
            pltpu.VMEM((n_dp, ff // wide, width // n_dp, wide), jnp.bfloat16),
            pltpu.VMEM((width, total), jnp.bfloat16),
            pltpu.VMEM((ff // wide, width, wide), jnp.bfloat16),
            dma((ff // wide,)), dma((ff // wide, n_dp)), dma((ff // wide, n_dp)),
        ],
        compiler_params=pltpu.CompilerParams(
            collective_id=2, has_side_effects=True, vmem_limit_bytes=56 * 1024 * 1024),
    )(rows, slope, spread, seq_dh)


def on_device(tokens, expert_ids, router, weight_in, weight_out, premises, positive, tile_mask):
    bf16, f32 = jnp.bfloat16, jnp.float32
    token_count, width = tokens.shape
    n_dp, n_ex = lax.axis_size("dp"), lax.axis_size("expert")
    blocks = n_dp * n_ex
    capacity = 4 * token_count // n_ex
    ff = weight_in.shape[2] // n_dp
    dp, ex = lax.axis_index("dp"), lax.axis_index("expert")
    device = dp * n_ex + ex
    per_dev = token_count // LEN
    seqs = blocks * per_dev

    all_tokens, gates, keys = gather(n_dp, n_ex, tokens, expert_ids, router, premises)
    keys = keys.reshape(n_dp * premises.shape[0], width)

    gate = gates[:, 0, :]
    named = gate != 0
    upper = (jnp.arange(token_count)[:, None] <= jnp.arange(token_count)[None, :]).astype(bf16)
    place_at = jnp.dot(named.astype(bf16), upper, preferred_element_type=f32).astype(jnp.int32) - 1
    place = jnp.logical_and(
        place_at[:, None, :] == jnp.arange(capacity, dtype=jnp.int32)[None, :, None], named[:, None, :]
    )
    rows = lax.dot_general(
        place.astype(bf16), all_tokens, (((2,), (1,)), ((0,), (0,))), preferred_element_type=f32
    ).astype(bf16).reshape(blocks * capacity, width)
    own_seq = (jnp.arange(token_count) // LEN)[:, None] == jnp.arange(per_dev)[None, :]
    slot_gate = jnp.sum(
        jnp.where(
            jnp.logical_and(place[:, :, :, None], own_seq[None, None]),
            gate[:, None, :, None],
            0.0,
        ),
        axis=2,
    )
    eye = jnp.eye(blocks, dtype=f32)
    spread = (slot_gate[:, :, None, :] * eye[:, None, :, None]).astype(bf16).reshape(
        blocks * capacity, seqs
    )

    w_in = lax.dynamic_slice_in_dim(weight_in[0], dp * ff, ff, 1)
    w_out = lax.dynamic_slice_in_dim(weight_out[0], dp * ff, ff, 0)
    pre_act = jnp.dot(rows, w_in, preferred_element_type=f32)
    gelu_val, slope_val = gelu_parts(pre_act)
    hidden, slope = gelu_val.astype(bf16), slope_val.astype(bf16)
    seq_hidden = lax.dot_general(
        spread, hidden, (((0,), (0,)), ((), ())), preferred_element_type=f32
    ).astype(bf16)
    partial = jnp.dot(seq_hidden, w_out, preferred_element_type=f32)
    own_sum = jnp.sum(tokens.astype(f32).reshape(per_dev, LEN, width), axis=1)
    key_scale = lax.rsqrt(jnp.sum(jnp.square(keys.astype(f32)), axis=1) + EPSILON)
    own_positive = lax.dynamic_slice_in_dim(positive, device * per_dev, per_dev)
    mask_row = lax.dynamic_index_in_dim(tile_mask, device, 0, keepdims=False)
    pos_hot = jnp.arange(keys.shape[0], dtype=jnp.int32)[None, :] == own_positive[:, None]
    include = jnp.logical_or(jnp.repeat(mask_row, premises.shape[0])[None, :] == 1, pos_hot)
    fill = ((0, 16 - per_dev), (0, 0))
    delta = loss_grads(
        n_dp, n_ex, partial.reshape(blocks, per_dev, width), own_sum, keys, key_scale[None, :],
        jnp.pad(include.astype(f32), fill), jnp.pad(pos_hot.astype(f32), fill),
    ).reshape(seqs, width).astype(bf16)

    grad_out = lax.dot_general(
        seq_hidden, delta, (((0,), (0,)), ((), ())), preferred_element_type=f32
    )
    seq_dh = lax.dot_general(
        delta, w_out, (((1,), (1,)), ((), ())), preferred_element_type=f32
    ).astype(bf16)
    grad_in = exchange(n_dp, rows, slope, spread, seq_dh)
    return (grad_in.astype(f32)[None], grad_out[None])


def solution(mesh):
    in_specs = (
        P(AXES, None),
        P(AXES, None),
        P(),
        P("expert", None, None),
        P("expert", None, None),
        P("dp", None),
        P(),
        P(),
    )
    out_specs = (P("expert", "dp", None), P("expert", "dp", None))
    return jax.shard_map(
        on_device, mesh=mesh, in_specs=in_specs, out_specs=out_specs, check_vma=False
    )
```

```python
import functools

import jax
import jax.numpy as jnp
from jax import lax
from jax.experimental import pallas as pl
from jax.experimental.pallas import tpu as pltpu
from jax.sharding import PartitionSpec as P

LEN = 64
SCORE_SCALE = 20.0
LOSS_SCALE = 64.0
EPSILON = 1e-06
AXES = ("dp", "expert")


def gelu_parts(pre_act):
    inner_arg = 0.7978845608028654 * (pre_act + 0.044715 * pre_act * pre_act * pre_act)
    tangent = jnp.tanh(inner_arg)
    gelu_val = 0.5 * pre_act * (1.0 + tangent)
    slope_val = 0.5 * (1.0 + tangent) + 0.5 * pre_act * (
        1.0 - tangent * tangent
    ) * 0.7978845608028654 * (1.0 + 0.134145 * pre_act * pre_act)
    return (gelu_val, slope_val)


MESH = pl.DeviceIdType.MESH


def greet_all(n_ex, blocks, me):
    barrier = pltpu.get_barrier_semaphore()

    def hello(d, _):
        t = lax.rem(me + d, blocks)
        pl.semaphore_signal(barrier, inc=1, device_id=(t // n_ex, lax.rem(t, n_ex)), device_id_type=MESH)
        return 0

    lax.fori_loop(1, blocks, hello, 0)
    pl.semaphore_wait(barrier, blocks - 1)


def gather_kernel(n_dp, n_ex, tok, tok_v, ids, router, prem, all_tok, gates, keys,
                  gmap, local_sem, send_sem, core_sem, recv_sem, gsend_sem, grecv_sem, psend_sem, precv_sem,
                  hsend_sem, hrecv_sem):
    blocks, nz = n_dp * n_ex, n_ex // 2
    i, e = lax.axis_index("dp"), lax.axis_index("expert")
    z, c = e // 2, lax.rem(e, 2)
    me, other = i * n_ex + e, z * 2 + (1 - c)

    def at_block(ii, zz, cc):
        return ii * n_ex + zz * 2 + cc

    def move(src, block, sem, device):
        return pltpu.make_async_remote_copy(
            src_ref=src, dst_ref=all_tok.at[block], send_sem=sem, recv_sem=recv_sem.at[block],
            device_id=device, device_id_type=MESH)

    greet_all(n_ex, blocks, me)

    own = pltpu.make_async_copy(tok, all_tok.at[me], local_sem.at[0])
    own.start()
    own_keys = pltpu.make_async_copy(prem, keys.at[i], local_sem.at[1])
    own_keys.start()

    square = n_dp == 4
    peers = 3 if square else n_dp

    def peer(d):
        if not square:
            return lax.rem(i + d, n_dp)
        return (2 - d) * (i + 1 - 2 * lax.rem(i, 2)) + (d - 1) * lax.rem(i + 2, 4)

    def own_dp(d, _):
        move(tok, me, send_sem.at[0, d], (peer(d), e)).start()
        return 0

    def own_z(k, _):
        move(tok, me, send_sem.at[k, 0], (i, lax.rem(z + k, nz) * 2 + c)).start()
        return 0

    lax.fori_loop(1, peers, own_dp, 0)
    lax.fori_loop(1, nz, own_z, 0)
    move(tok, me, core_sem.at[me], (i, other)).start()

    experts = router.shape[0]
    logits = lax.dot_general(
        router[...], tok_v[...], (((1,), (1,)), ((), ())), preferred_element_type=jnp.float32)
    lane = lax.broadcasted_iota(jnp.int32, logits.shape, 0)
    hot0, hot1 = lane == ids[0:1, :], lane == ids[1:2, :]
    picked0 = jnp.sum(jnp.where(hot0, logits, 0.0), axis=0, keepdims=True)
    picked1 = jnp.sum(jnp.where(hot1, logits, 0.0), axis=0, keepdims=True)
    gate0, gate1 = jax.nn.sigmoid(picked0 - picked1), jax.nn.sigmoid(picked1 - picked0)
    table = jnp.where(hot0, gate0, jnp.where(hot1, gate1, 0.0)).astype(jnp.bfloat16).astype(jnp.float32)
    for k in range(experts):
        gmap[k] = jnp.broadcast_to(table[k:k + 1, :], gmap.shape[1:])

    def gate_copy(d):
        t = lax.rem(me + d, blocks)
        return pltpu.make_async_remote_copy(
            src_ref=gmap.at[lax.rem(t, n_ex)], dst_ref=gates.at[me], send_sem=gsend_sem.at[d],
            recv_sem=grecv_sem.at[me], device_id=(t // n_ex, lax.rem(t, n_ex)), device_id_type=MESH)

    def gate_start(d, _):
        gate_copy(d).start()
        return 0

    lax.fori_loop(1, blocks, gate_start, 0)
    own_gate = pltpu.make_async_copy(gmap.at[e], gates.at[me], local_sem.at[2])
    own_gate.start()

    def from_z(k, _):
        block = at_block(i, lax.rem(z + k, nz), c)
        move(tok, block, send_sem.at[0, 0], (i, e)).wait_recv()

        def on(d, _):
            move(all_tok.at[block], block, send_sem.at[k, d], (peer(d), e)).start()
            return 0

        lax.fori_loop(1, peers, on, 0)
        move(all_tok.at[block], block, core_sem.at[block], (i, other)).start()
        return 0

    def half_block(block, part, device, k):
        rows = all_tok.at[block, pl.ds(part * (tok.shape[0] // 2), tok.shape[0] // 2), :]
        return pltpu.make_async_remote_copy(
            src_ref=rows, dst_ref=rows, send_sem=hsend_sem.at[k, part], recv_sem=hrecv_sem.at[block, part],
            device_id=device, device_id_type=MESH)

    def from_dp(n, _):
        k, d = n // (peers - 1), 1 + lax.rem(n, peers - 1)
        block = at_block(peer(d), lax.rem(z + k, nz), c)
        move(tok, block, send_sem.at[0, 0], (i, e)).wait_recv()
        if square:
            half_block(block, d - 1, (peer(3 - d), e), k).start()
        move(all_tok.at[block], block, core_sem.at[block], (i, other)).start()
        return 0

    lax.fori_loop(0, peers - 1, from_dp, 0)
    lax.fori_loop(1, nz, from_z, 0)

    def half(src, row, part, sem, device):
        return pltpu.make_async_remote_copy(
            src_ref=src, dst_ref=keys.at[row, part], send_sem=psend_sem.at[sem],
            recv_sem=precv_sem.at[row, part], device_id=device, device_id_type=MESH)

    def own_half(d, _):
        half(prem.at[c], i, c, d, (lax.rem(i + d, n_dp), e)).start()
        return 0

    lax.fori_loop(1, n_dp, own_half, 0)

    lax.fori_loop(peers - 1, nz * (peers - 1), from_dp, 0)

    def from_diagonal(k, _):
        block = at_block(3 - i, lax.rem(z + k, nz), c)
        half_block(block, 0, (i, e), k).wait_recv()
        half_block(block, 1, (i, e), k).wait_recv()
        move(all_tok.at[block], block, core_sem.at[block], (i, other)).start()
        return 0

    if square:
        lax.fori_loop(0, nz, from_diagonal, 0)

    def hand_half(d, _):
        row = lax.rem(i + d, n_dp)
        half(prem.at[c], row, c, d, (i, e)).wait_recv()
        half(keys.at[row, c], row, c, n_dp + d, (i, other)).start()
        return 0

    lax.fori_loop(1, n_dp, hand_half, 0)

    own.wait()
    own_keys.wait()
    own_gate.wait()

    def end_core(n, _):
        ii, zz = n // nz, lax.rem(n, nz)
        move(tok, at_block(ii, zz, 1 - c), send_sem.at[0, 0], (i, e)).wait_recv()
        move(tok, me, core_sem.at[at_block(ii, zz, c)], (i, e)).wait_send()
        return 0

    lax.fori_loop(0, n_dp * nz, end_core, 0)

    def end_dp(n, _):
        move(tok, me, send_sem.at[n // (peers - 1), 1 + lax.rem(n, peers - 1)], (i, e)).wait_send()
        return 0

    def end_z(k, _):
        move(tok, me, send_sem.at[k, 0], (i, e)).wait_send()
        return 0

    def end_diagonal(k, _):
        half_block(me, 0, (i, e), k).wait_send()
        half_block(me, 1, (i, e), k).wait_send()
        return 0

    lax.fori_loop(0, nz * (peers - 1), end_dp, 0)
    lax.fori_loop(1, nz, end_z, 0)
    if square:
        lax.fori_loop(0, nz, end_diagonal, 0)

    def end_half(d, _):
        half(prem.at[c], lax.rem(i + d, n_dp), 1 - c, d, (i, e)).wait_recv()
        half(prem.at[c], i, c, d, (i, e)).wait_send()
        half(prem.at[c], i, c, n_dp + d, (i, e)).wait_send()
        return 0

    lax.fori_loop(1, n_dp, end_half, 0)

    def end_gate(d, _):
        s = lax.rem(me + d, blocks)
        gate_copy(d).wait_send()
        pltpu.make_async_remote_copy(
            src_ref=gmap.at[0], dst_ref=gates.at[s], send_sem=gsend_sem.at[d],
            recv_sem=grecv_sem.at[s], device_id=(i, e), device_id_type=MESH).wait_recv()
        return 0

    lax.fori_loop(1, blocks, end_gate, 0)


def gather(n_dp, n_ex, tokens, ids, router, premises):
    blocks = n_dp * n_ex
    tok, width = tokens.shape
    prem = premises.reshape(2, premises.shape[0] // 2, width)
    any_spec, vmem = pl.BlockSpec(memory_space=pl.ANY), pl.BlockSpec(memory_space=pltpu.VMEM)
    dma = pltpu.SemaphoreType.DMA
    return pl.pallas_call(
        functools.partial(gather_kernel, n_dp, n_ex),
        out_shape=(
            jax.ShapeDtypeStruct((blocks, tok, width), tokens.dtype),
            jax.ShapeDtypeStruct((blocks, 8, tok), jnp.float32),
            jax.ShapeDtypeStruct((n_dp,) + prem.shape, premises.dtype),
        ),
        in_specs=[any_spec, vmem, vmem, vmem, any_spec],
        out_specs=(any_spec, any_spec, any_spec),
        scratch_shapes=[
            pltpu.VMEM((router.shape[1], 8, tok), jnp.float32),
            dma((3,)), dma((n_ex // 2, n_dp)), dma((blocks,)), dma((blocks,)),
            dma((blocks,)), dma((blocks,)), dma((2 * n_dp,)), dma((n_dp, 2)),
            dma((n_ex // 2, 2)), dma((blocks, 2)),
        ],
        compiler_params=pltpu.CompilerParams(collective_id=0, has_side_effects=True),
    )(tokens, tokens, ids.T, router.T, prem)


def loss_kernel(n_dp, n_ex, partial, own_sum, keys, key_scale, include, pos_hot, out,
                inbox, ssend, srecv, gsend, grecv):
    blocks = n_dp * n_ex
    i, e = lax.axis_index("dp"), lax.axis_index("expert")
    me = i * n_ex + e
    per_dev, width = own_sum.shape

    def copy(src, dst, slot, send, recv, t, s):
        return pltpu.make_async_remote_copy(
            src_ref=src, dst_ref=dst.at[slot], send_sem=send.at[s], recv_sem=recv.at[slot],
            device_id=(t // n_ex, lax.rem(t, n_ex)), device_id_type=MESH)

    greet_all(n_ex, blocks, me)

    def scatter(d, _):
        t = lax.rem(me + d, blocks)
        copy(partial.at[t], inbox, me, ssend, srecv, t, d).start()
        return 0

    lax.fori_loop(1, blocks, scatter, 0)

    def collect(d, total):
        s = lax.rem(me + d, blocks)
        copy(partial.at[me], inbox, s, ssend, srecv, me, d).wait_recv()
        return total + inbox[s]

    total = lax.fori_loop(1, blocks, collect, partial[me] + own_sum[...])
    pad = include.shape[0]
    pooled = jnp.concatenate([total, jnp.zeros((pad - per_dev, width), jnp.float32)], axis=0) / LEN
    row_scale = lax.rsqrt(jnp.sum(pooled * pooled, axis=1, keepdims=True) + EPSILON)
    unit = pooled * row_scale
    rows = keys[...]
    scores = SCORE_SCALE * lax.dot_general(
        unit.astype(jnp.bfloat16), rows, (((1,), (1,)), ((), ())), preferred_element_type=jnp.float32
    ) * key_scale[...]
    exp_scores = jnp.where(include[...] > 0, jnp.exp(scores), 0.0)
    partition = jnp.sum(exp_scores, axis=1, keepdims=True)
    soft = (exp_scores * key_scale[...]).astype(jnp.bfloat16)
    weighted = jnp.dot(soft, rows, preferred_element_type=jnp.float32)
    hot = pos_hot[...]
    pos_vec = jnp.dot(hot.astype(jnp.bfloat16), rows, preferred_element_type=jnp.float32)
    pos_scale = jnp.sum(hot * key_scale[...], axis=1, keepdims=True)
    delta_unit = LOSS_SCALE * SCORE_SCALE * (weighted / partition - pos_vec * pos_scale)
    delta = row_scale * (delta_unit - unit * jnp.sum(unit * delta_unit, axis=1, keepdims=True))
    out[me] = delta[:per_dev] / LEN

    def spread(d, _):
        t = lax.rem(me + d, blocks)
        copy(out.at[me], out, me, gsend, grecv, t, d).start()
        return 0

    lax.fori_loop(1, blocks, spread, 0)

    def end(d, _):
        s = lax.rem(me + d, blocks)
        copy(out.at[me], out, s, gsend, grecv, me, d).wait_recv()
        copy(out.at[me], out, me, gsend, grecv, s, d).wait_send()
        copy(partial.at[s], inbox, me, ssend, srecv, s, d).wait_send()
        return 0

    lax.fori_loop(1, blocks, end, 0)


def loss_grads(n_dp, n_ex, partial, own_sum, keys, key_scale, include, pos_hot):
    blocks = n_dp * n_ex
    vmem = pl.BlockSpec(memory_space=pltpu.VMEM)
    dma = pltpu.SemaphoreType.DMA
    return pl.pallas_call(
        functools.partial(loss_kernel, n_dp, n_ex),
        out_shape=jax.ShapeDtypeStruct(partial.shape, jnp.float32),
        in_specs=[vmem] * 6,
        out_specs=vmem,
        scratch_shapes=[
            pltpu.VMEM(partial.shape, jnp.float32),
            dma((blocks,)), dma((blocks,)), dma((blocks,)), dma((blocks,)),
        ],
        compiler_params=pltpu.CompilerParams(
            collective_id=1, has_side_effects=True, vmem_limit_bytes=48 * 1024 * 1024),
    )(partial, own_sum, keys, key_scale, include, pos_hot)


def exchange_kernel(n_dp, rows, slope, spread, seq_dh, grads, out, turned, part, local_sem, send_sem, recv_sem):
    i, e = lax.axis_index("dp"), lax.axis_index("expert")
    _, parts, keep, wide = out.shape
    total, width = rows.shape
    step = 256

    barrier = pltpu.get_barrier_semaphore()
    for d in range(1, n_dp):
        pl.semaphore_signal(barrier, inc=1, device_id=(lax.rem(i + d, n_dp), e), device_id_type=MESH)

    def turn(n, _):
        at = pl.multiple_of(n * step, step)
        turned[:, pl.ds(at, step)] = rows[pl.ds(at, step), :].T
        return 0

    lax.fori_loop(0, total // step, turn, 0)
    pl.semaphore_wait(barrier, n_dp - 1)

    def copy(f, d, slot):
        t = lax.rem(i + d, n_dp)
        return pltpu.make_async_remote_copy(
            src_ref=part.at[f, pl.ds(pl.multiple_of(t * keep, keep), keep), :],
            dst_ref=out.at[slot, f], send_sem=send_sem.at[f, d], recv_sem=recv_sem.at[f, slot],
            device_id=(t, e), device_id_type=MESH)

    for f in range(parts):
        cols = slice(f * wide, (f + 1) * wide)
        back = jnp.dot(spread[...], seq_dh[:, cols], preferred_element_type=jnp.float32)
        delta_pre = (back * slope[:, cols].astype(jnp.float32)).astype(jnp.bfloat16)
        part[f] = jnp.dot(
            turned[...], delta_pre, preferred_element_type=jnp.float32).astype(jnp.bfloat16)
        for d in range(1, n_dp):
            copy(f, d, i).start()
        pltpu.make_async_copy(
            part.at[f, pl.ds(pl.multiple_of(i * keep, keep), keep), :], out.at[i, f], local_sem.at[f]
        ).start()
    for f in range(parts):
        pltpu.make_async_copy(
            part.at[f, pl.ds(pl.multiple_of(i * keep, keep), keep), :], out.at[i, f], local_sem.at[f]
        ).wait()
        for d in range(1, n_dp):
            copy(f, d, lax.rem(i + d, n_dp)).wait_recv()
        for j in range(n_dp):
            at = (j * parts + f) * wide
            grads[:, at:at + wide] = out[j, f]
    for f in range(parts):
        for d in range(1, n_dp):
            copy(f, d, i).wait_send()


def exchange(n_dp, rows, slope, spread, seq_dh):
    total, width = rows.shape
    ff = slope.shape[1]
    wide = 256 if ff % 256 == 0 else ff
    vmem = pl.BlockSpec(memory_space=pltpu.VMEM)
    dma = pltpu.SemaphoreType.DMA
    return pl.pallas_call(
        functools.partial(exchange_kernel, n_dp),
        out_shape=jax.ShapeDtypeStruct((width // n_dp, n_dp * ff), jnp.bfloat16),
        in_specs=[vmem] * 4,
        out_specs=vmem,
        scratch_shapes=[
            pltpu.VMEM((n_dp, ff // wide, width // n_dp, wide), jnp.bfloat16),
            pltpu.VMEM((width, total), jnp.bfloat16),
            pltpu.VMEM((ff // wide, width, wide), jnp.bfloat16),
            dma((ff // wide,)), dma((ff // wide, n_dp)), dma((ff // wide, n_dp)),
        ],
        compiler_params=pltpu.CompilerParams(
            collective_id=2, has_side_effects=True, vmem_limit_bytes=56 * 1024 * 1024),
    )(rows, slope, spread, seq_dh)


def on_device(tokens, expert_ids, router, weight_in, weight_out, premises, positive, tile_mask):
    bf16, f32 = jnp.bfloat16, jnp.float32
    token_count, width = tokens.shape
    n_dp, n_ex = lax.axis_size("dp"), lax.axis_size("expert")
    blocks = n_dp * n_ex
    capacity = 4 * token_count // n_ex
    ff = weight_in.shape[2] // n_dp
    dp, ex = lax.axis_index("dp"), lax.axis_index("expert")
    device = dp * n_ex + ex
    per_dev = token_count // LEN
    seqs = blocks * per_dev

    all_tokens, gates, keys = gather(n_dp, n_ex, tokens, expert_ids, router, premises)
    keys = keys.reshape(n_dp * premises.shape[0], width)

    gate = gates[:, 0, :]
    named = gate != 0
    upper = (jnp.arange(token_count)[:, None] <= jnp.arange(token_count)[None, :]).astype(bf16)
    place_at = jnp.dot(named.astype(bf16), upper, preferred_element_type=f32).astype(jnp.int32) - 1
    place = jnp.logical_and(
        place_at[:, None, :] == jnp.arange(capacity, dtype=jnp.int32)[None, :, None], named[:, None, :]
    )
    rows = lax.dot_general(
        place.astype(bf16), all_tokens, (((2,), (1,)), ((0,), (0,))), preferred_element_type=f32
    ).astype(bf16).reshape(blocks * capacity, width)
    own_seq = (jnp.arange(token_count) // LEN)[:, None] == jnp.arange(per_dev)[None, :]
    slot_gate = jnp.sum(
        jnp.where(
            jnp.logical_and(place[:, :, :, None], own_seq[None, None]),
            gate[:, None, :, None],
            0.0,
        ),
        axis=2,
    )
    eye = jnp.eye(blocks, dtype=f32)
    spread = (slot_gate[:, :, None, :] * eye[:, None, :, None]).astype(bf16).reshape(
        blocks * capacity, seqs
    )

    w_in = lax.dynamic_slice_in_dim(weight_in[0], dp * ff, ff, 1)
    w_out = lax.dynamic_slice_in_dim(weight_out[0], dp * ff, ff, 0)
    pre_act = jnp.dot(rows, w_in, preferred_element_type=f32)
    gelu_val, slope_val = gelu_parts(pre_act)
    hidden, slope = lax.optimization_barrier((gelu_val.astype(bf16), slope_val.astype(bf16)))
    seq_hidden = lax.dot_general(
        spread, hidden, (((0,), (0,)), ((), ())), preferred_element_type=f32
    ).astype(bf16)
    partial = jnp.dot(seq_hidden, w_out, preferred_element_type=f32)
    own_sum = jnp.sum(tokens.astype(f32).reshape(per_dev, LEN, width), axis=1)
    key_scale = lax.rsqrt(jnp.sum(jnp.square(keys.astype(f32)), axis=1) + EPSILON)
    own_positive = lax.dynamic_slice_in_dim(positive, device * per_dev, per_dev)
    mask_row = lax.dynamic_index_in_dim(tile_mask, device, 0, keepdims=False)
    pos_hot = jnp.arange(keys.shape[0], dtype=jnp.int32)[None, :] == own_positive[:, None]
    include = jnp.logical_or(jnp.repeat(mask_row, premises.shape[0])[None, :] == 1, pos_hot)
    fill = ((0, 16 - per_dev), (0, 0))
    delta = loss_grads(
        n_dp, n_ex, partial.reshape(blocks, per_dev, width), own_sum, keys, key_scale[None, :],
        jnp.pad(include.astype(f32), fill), jnp.pad(pos_hot.astype(f32), fill),
    ).reshape(seqs, width).astype(bf16)

    grad_out = lax.dot_general(
        seq_hidden, delta, (((0,), (0,)), ((), ())), preferred_element_type=f32
    )
    seq_dh = lax.dot_general(
        delta, w_out, (((1,), (1,)), ((), ())), preferred_element_type=f32
    ).astype(bf16)
    grad_in = exchange(n_dp, rows, slope, spread, seq_dh)
    return (grad_in.astype(f32)[None], grad_out[None])


def solution(mesh):
    in_specs = (
        P(AXES, None),
        P(AXES, None),
        P(),
        P("expert", None, None),
        P("expert", None, None),
        P("dp", None),
        P(),
        P(),
    )
    out_specs = (P("expert", "dp", None), P("expert", "dp", None))
    return jax.shard_map(
        on_device, mesh=mesh, in_specs=in_specs, out_specs=out_specs, check_vma=False
    )
```
